512 devices in a mesh: lev: 16 (over z), lat: 32 (over x, y, core).
Axes of the slice: x: 4, y: 4, z: 16, core: 2. Of those that a mesh axis runs over, the one named last changes fastest.
Arguments:
- adjoint_in: float32 [2, 32, 512, 1024], P(None, 'lev', 'lat'), may hold values from -6 to 6
- courant: float32 [2, 32, 512, 1024], P(None, None, 'lat', 'lev'), may hold values from -0.6 to 0.6
- cloud_top: int32 [512, 1024], P('lat', 'lev'), may hold values from 0 to 15
- conv_inverse: float32 [16, 32, 32], replicated
- sounding_kernel: float32 [16, 32, 512, 64], P('lev', 'lat'), may hold values from -6 to 6
- sounding_weight: float32 [16, 32, 512, 2], P('lev', 'lat'), may hold values from -6 to 6
- sounding_owner: int32 [16, 32, 512], P('lev', 'lat'), may hold values from 0 to 31, as said below
- sounding_cell: int32 [16, 32, 512], P('lev', 'lat'), may hold values from 0 to 1023
- sounding_count: int32 [16, 32], P('lev', 'lat'), may hold values from 384 to 512
Outputs:
- adjoint_out: float32 [2, 32, 512, 1024], P(None, 'lev', 'lat')
- sensitivity: float32 [16, 32, 512, 2], P('lev', 'lat')
The draws below stay inside these ranges and needn't reach their ends.
Inputs may be any that keep to these rules, and one draw needn't show every extreme that they name: `sounding_owner`: of the sounding slots of one device, at most 48 name any one band.
All inputs are finite; a program needn't handle non-finite values.
Results may differ from the reference program's by a relative error of at most 0.0003.
Values sent between devices are 32-bit elements; how exact they have to be, the bound alone decides.
A program may use at most 64 MiB of HBM per device.

```python
import jax
import jax.numpy as jnp
from jax import lax

LAT_DEV = 16
LON = 1024
S_DEV = 512
NTOP = 16
K = 32
LAT = 512
COLS_OWN = 1024
N_LEV = 16
N_LAT = 32


def draw_conv_inverse(key, part):
    key = jax.random.fold_in(key, 11)
    key_diag, key_off = jax.random.split(key)
    diagonal_part = jax.random.uniform(key_diag, (NTOP, K), jnp.float32, 0.6, 1.4)
    off_part = jax.random.normal(key_off, (NTOP, K, K), jnp.float32) * (0.4 / K ** 0.5)
    identity = jnp.eye(K, dtype=jnp.float32)
    return off_part * (1.0 - identity) + identity * diagonal_part[:, :, None]


def draw_sounding_owner(key, part):
    key = jax.random.fold_in(key, 5)
    capacity = 3 * S_DEV // N_LAT
    slots_all = N_LAT * capacity
    key_busy, key_rest = jax.random.split(key)
    busy = jax.random.randint(key_busy, (N_LEV,), 0, N_LAT)
    busy_each = jnp.repeat(busy, N_LAT)
    device_keys = jax.random.split(key_rest, N_LEV * N_LAT)

    def one_device(dev_key, busy_band):
        key_score, key_mix = jax.random.split(dev_key)
        labels = jnp.arange(slots_all, dtype=jnp.int32) // capacity
        scores = jax.random.randint(key_score, (slots_all,), 0, 65536)
        scores = jnp.where(labels == busy_band, scores - 131072, scores)
        scores = scores * slots_all + jnp.arange(slots_all, dtype=jnp.int32)
        order = jnp.argsort(scores)
        chosen = labels[order][:S_DEV]
        half_len = S_DEV // 2
        mixing = jax.random.permutation(key_mix, half_len)
        return jnp.concatenate([chosen[:half_len][mixing], chosen[half_len:]])
    owners = jax.vmap(one_device)(device_keys, busy_each)
    return owners.reshape(N_LEV, N_LAT, S_DEV).astype(jnp.int32)


def draw_sounding_count(key, part):
    key = jax.random.fold_in(key, 9)
    key_held, key_full = jax.random.split(key)
    held = jax.random.randint(key_held, (N_LEV * N_LAT,), 3 * S_DEV // 4, S_DEV + 1)
    full_dev = jax.random.randint(key_full, (), 0, N_LEV * N_LAT)
    held = jnp.where(jnp.arange(N_LEV * N_LAT) == full_dev, S_DEV, held)
    return held.reshape(N_LEV, N_LAT).astype(jnp.int32)


def touch_ends(drawn, rng, least, high):
    longest = drawn.shape.index(max(drawn.shape))
    spots = []
    for shift in (0, 1):
        where = [jax.random.randint(jax.random.fold_in(rng, axis), (), 0, length) for axis, length in enumerate(drawn.shape)]
        where[longest] = (where[longest] + shift) % drawn.shape[longest]
        spots.append(tuple(where))
    return drawn.at[spots[0]].set(least).at[spots[1]].set(high)


def block_scale(key, dims, pieces, smallest, high):
    def one(axis_at, shards_of):
        steps = jax.random.uniform(jax.random.fold_in(jax.random.fold_in(key, 6), axis_at), (shards_of,), jnp.float32, smallest / len(pieces), high / len(pieces))
        return jnp.repeat(jnp.exp(steps), dims[axis_at] // shards_of).reshape((-1,) + (1,) * (len(dims) - axis_at - 1))

    gain = one(*pieces[0])
    for cut in pieces[1:]:
        gain = gain * one(*cut)
    return gain


def scatter_about(key, shape, scale, most, cuts=(), kind=jnp.bfloat16):
    drawn = jax.random.normal(key, shape, jnp.float32) * scale
    if len(cuts) > 0:
        drawn = block_scale(key, shape, cuts, -0.22, 0.18) * drawn
    return jnp.clip(drawn, min=-most, max=most).astype(kind)


def setup_inputs(seed: int = 0) -> dict:
    key_list = jax.random.split(jax.random.key(seed), 10)
    adjoint_in = scatter_about(key_list[0], (2, K, LAT, LON), 1.0, 6.0, ((1, 16), (2, 32)), jnp.float32)
    courant = jnp.clip(jax.random.uniform(key_list[1], (2, K, LAT, LON), jnp.float32, -0.6, 0.6) * block_scale(key_list[1], (2, K, LAT, LON), ((2, 32), (3, 16)), -0.4, 0.0), -0.6, 0.6)
    cloud_top = touch_ends(jax.random.randint(key_list[2], (LAT, LON), 0, NTOP), jax.random.fold_in(key_list[2], 1), 0, NTOP - 1).astype(jnp.int32)
    conv_inverse = draw_conv_inverse(jax.random.fold_in(key_list[9], 71), 0)
    sounding_kernel = scatter_about(key_list[4], (N_LEV, N_LAT, S_DEV, 2 * K), 1.0, 6.0, ((0, 16), (1, 32)), jnp.float32)
    sounding_weight = scatter_about(key_list[5], (N_LEV, N_LAT, S_DEV, 2), 1.0, 6.0, ((0, 16), (1, 32)), jnp.float32)
    sounding_owner = draw_sounding_owner(jax.random.fold_in(key_list[9], 71), 0)
    sounding_cell = touch_ends(jax.random.randint(key_list[7], (N_LEV, N_LAT, S_DEV), 0, COLS_OWN), jax.random.fold_in(key_list[7], 1), 0, COLS_OWN - 1).astype(jnp.int32)
    sounding_count = draw_sounding_count(jax.random.fold_in(key_list[9], 71), 0)
    return {"adjoint_in": adjoint_in, "courant": courant, "cloud_top": cloud_top, "conv_inverse": conv_inverse, "sounding_kernel": sounding_kernel, "sounding_weight": sounding_weight, "sounding_owner": sounding_owner, "sounding_cell": sounding_cell, "sounding_count": sounding_count}


def trim(array, along, start, length):
    return lax.slice_in_dim(array, start, start + length, axis=along % array.ndim)

def face_flux(field, cour, along, extent):
    back_two = trim(field, along, 0, extent + 5)
    back_one = trim(field, along, 1, extent + 5)
    center = trim(field, along, 2, extent + 5)
    ahead = trim(field, along, 3, extent + 5)
    speed = trim(cour, along, 1, extent + 5)
    upwind = speed * (back_one + 0.25 * (1.0 - speed) * (center - back_two))
    downwind = speed * (center - 0.25 * (1.0 + speed) * (ahead - back_one))
    return jnp.where(speed >= 0.0, upwind, downwind)

def forward_step(field, cour_x, cour_y, lat_count, lon_count):
    rows_x = trim(field, -2, 2, lat_count + 4)
    speed_x = trim(cour_x, -2, 1, lat_count + 4)
    flux_x = face_flux(rows_x, speed_x, -1, lon_count)
    div_x = trim(flux_x, -1, 1, lon_count + 4) - trim(flux_x, -1, 0, lon_count + 4)
    cols_y = trim(field, -1, 2, lon_count + 4)
    speed_y = trim(cour_y, -1, 1, lon_count + 4)
    flux_y = face_flux(cols_y, speed_y, -2, lat_count)
    div_y = trim(flux_y, -2, 1, lat_count + 4) - trim(flux_y, -2, 0, lat_count + 4)
    center = trim(trim(field, -2, 2, lat_count + 4), -1, 2, lon_count + 4)
    return center - div_x - div_y

def adjoint_step(adj_inner, cour_x, cour_y, lat_count, lon_count):
    shape_full = adj_inner.shape[:-2] + (lat_count + 8, lon_count + 8)
    start = jnp.zeros(shape_full, adj_inner.dtype)
    _, pullback = jax.vjp(lambda field: forward_step(field, cour_x, cour_y, lat_count, lon_count), start)
    grad_field = pullback(adj_inner)[0]
    return grad_field[..., 4:lat_count + 4, 4:lon_count + 4]

def local_adjoint(padded, global_row, lat_total):
    inside = (global_row >= 0) & (global_row < lat_total)
    keep_row = inside[:, None]
    adj_all = jnp.where(keep_row, padded[0:2], 0.0)
    cour_x = jnp.where(keep_row, padded[2], 0.0)
    cour_y = jnp.where(keep_row & (global_row != 0)[:, None], padded[3], 0.0)
    lat_count = padded.shape[-2] - 6
    lon_count = padded.shape[-1] - 6
    return adjoint_step(adj_all[..., 1:-1, 1:-1], cour_x, cour_y, lat_count, lon_count)

def reference(adjoint_in, courant, cloud_top, conv_inverse, sounding_kernel, sounding_weight, sounding_owner, sounding_cell, sounding_count):
    sector = LON // N_LEV
    total = LAT * LON
    is_valid = jnp.arange(S_DEV, dtype=jnp.int32)[None, None, :] < sounding_count[:, :, None]
    lev_of = jnp.arange(N_LEV, dtype=jnp.int32)[:, None, None]
    lat_row = sounding_owner * LAT_DEV + sounding_cell // sector
    lon_col = lev_of * sector + sounding_cell % sector
    column = jnp.where(is_valid, lat_row * LON + lon_col, total).reshape(-1).astype(jnp.int32)
    kernels = sounding_kernel.reshape(-1, 2, K)
    weights = sounding_weight.reshape(-1, 2)
    deposit = jax.ops.segment_sum(weights[:, :, None] * kernels, column, num_segments=total + 1)[:total]
    adj_mixed = adjoint_in.reshape(2, K, total) + jnp.transpose(deposit, (1, 2, 0))
    tops = cloud_top.reshape(total)

    def mix_class(top_class, running):
        matrix = lax.dynamic_index_in_dim(conv_inverse, top_class, 0, keepdims=False)
        mixed = jnp.einsum('kj,tkn->tjn', matrix, adj_mixed, precision=lax.Precision.HIGHEST)
        return running + jnp.where(tops[None, None, :] == top_class, mixed, 0.0)
    adj_conv = lax.fori_loop(0, NTOP, mix_class, jnp.zeros((2, K, total), jnp.float32))
    picked = jnp.take(adj_conv, jnp.minimum(column, total - 1), axis=2)
    sens_rows = jnp.einsum('mtk,tkm->mt', kernels, picked, precision=lax.Precision.HIGHEST)
    sens_rows = jnp.where(is_valid.reshape(-1)[:, None], sens_rows, 0.0)
    sensitivity = sens_rows.reshape(N_LEV, N_LAT, S_DEV, 2)
    stacked = jnp.concatenate([adj_conv.reshape(2, K, LAT, LON), courant], axis=0)
    stacked = jnp.pad(stacked, ((0, 0), (0, 0), (3, 3), (0, 0)))
    stacked = jnp.concatenate([stacked[..., -3:], stacked, stacked[..., :3]], axis=3)
    global_row = jnp.arange(LAT + 6, dtype=jnp.int32) - 3
    per_level = jnp.transpose(stacked, (1, 0, 2, 3))
    result = lax.map(lambda level_block: local_adjoint(level_block, global_row, LAT), per_level)
    adjoint_out = jnp.transpose(result, (1, 0, 2, 3))
    return (adjoint_out, sensitivity)
```

```python
import functools

import jax
import jax.numpy as jnp
from jax import lax
from jax.experimental import pallas as pl
from jax.experimental.pallas import tpu as pltpu
from jax.sharding import PartitionSpec as P

MESH = pl.DeviceIdType.MESH
F32, BF16, I32 = jnp.float32, jnp.bfloat16, jnp.int32
ROWS = 16
TILES = 8
HALF = 64
MSG = 8


def lanes(shape):
    return lax.broadcasted_iota(I32, shape, len(shape) - 1)


def turn(x, shift):
    shift = shift % 128
    return x if shift == 0 else pltpu.roll(x, shift, x.ndim - 1)


def low_half(shape):
    return lanes(shape) < HALF


def pair(a, b):
    low = low_half(a.shape)
    return jnp.where(low, a, turn(b, HALF)), jnp.where(low, turn(a, HALF), b)


def split(x):
    high = x.astype(BF16)
    return high, (x - high.astype(F32)).astype(BF16)


def dot(a, b, contract=(1, 0)):
    return lax.dot_general(
        a, b, (((contract[0],), (contract[1],)), ((), ())), preferred_element_type=F32
    )


def one_hot(mask):
    return jnp.where(mask, 1.0, 0.0).astype(BF16)


def pack_lon(tiles):
    x = lanes(tiles[0].shape) % HALF
    to_west, to_east = tiles[0], turn(tiles[0], 66)
    for p in range(1, TILES):
        here = x // 2 == p
        to_west = jnp.where(here, turn(tiles[p], 2 * p), to_west)
        to_east = jnp.where(here, turn(tiles[p], 2 * p + 66), to_east)
    return to_west, to_east


def shift_lon(tile, p, from_west, from_east, steps):
    x = lanes(tile.shape) % HALF
    east = turn(from_east, HALF - 2 * p)
    west = turn(from_west, 126 - 2 * p)
    out = []
    for d in steps:
        if d > 0:
            out.append(turn(jnp.where(x < d, east, tile), -d))
        else:
            out.append(turn(jnp.where(x >= HALF + d, west, tile), -d))
    return out


def pack_lat(tiles):
    low = low_half(tiles[0].shape)
    to_south = jnp.where(low, tiles[0], turn(tiles[1], HALF))
    to_north = jnp.where(low, turn(tiles[6], HALF), tiles[7])
    return to_south, to_north


def extend_lat(tiles, from_south, from_north):
    low = low_half(tiles[0].shape)
    return (
        [
            jnp.where(low, from_south, turn(tiles[6], HALF)),
            turn(jnp.where(low, tiles[7], from_south), HALF),
        ]
        + list(tiles)
        + [
            turn(jnp.where(low, from_north, tiles[0]), HALF),
            jnp.where(low, turn(tiles[1], HALF), from_north),
        ]
    )


def face_weights(before, here, after, after2):
    def parts(c):
        pos, neg = jnp.maximum(c, 0.0), jnp.minimum(c, 0.0)
        return pos, neg, 0.25 * pos * (1.0 - pos), 0.25 * neg * (1.0 + neg)

    _, _, _, sn_before = parts(before)
    _, neg_here, sp_here, _ = parts(here)
    pos_after, _, _, sn_after = parts(after)
    _, _, sp_after2, _ = parts(after2)
    own = neg_here + sp_here
    nxt = pos_after + sn_after
    return sn_before, -own - sn_before, own - nxt, nxt + sp_after2, -sp_after2


def kernel(
    n_lev,
    n_lat,
    adj_hbm,
    cour_hbm,
    top_hbm,
    mat_hbm,
    kern_hbm,
    wt_hbm,
    owner_hbm,
    cell_hbm,
    count_hbm,
    out_hbm,
    sens_hbm,
    adj_in,
    cour_in,
    top_in,
    mat_in,
    kern_in,
    wt_in,
    owner_in,
    cell_in,
    count_in,
    out_vm,
    sens_vm,
    fwd_out,
    fwd_in,
    back_out,
    back_in,
    msg_out,
    msg_in,
    ret_out,
    ret_in,
    c_lon_out,
    c_lon_in,
    c_lat_out,
    c_lat_in,
    a_lon_out,
    a_lon_in,
    a_lat_out,
    a_lat_in,
    place,
    payload,
    kern_rows,
    weighted,
    hot,
    deposit,
    cour_t,
    weights,
    mix,
    conv,
    conv_split,
    ret_split,
    in_sem,
    out_sem,
    fwd_send,
    fwd_recv,
    back_send,
    back_recv,
    msg_send,
    msg_recv,
    ret_send,
    ret_recv,
    c_send,
    c_recv,
    a_send,
    a_recv,
):
    lev, lat = lax.axis_index("lev"), lax.axis_index("lat")
    levels = 2 * n_lev
    slots = owner_in.shape[1]

    def lev_at(d):
        return lax.rem(lev + d + n_lev, n_lev)

    def lat_at(d):
        return lax.rem(lat + d + n_lat, n_lat)

    loads = [
        pltpu.make_async_copy(source, target, in_sem.at[i])
        for i, (source, target) in enumerate(
            [
                (adj_hbm, adj_in),
                (owner_hbm, owner_in),
                (cell_hbm, cell_in),
                (count_hbm, count_in),
                (kern_hbm, kern_in),
                (wt_hbm, wt_in),
                (cour_hbm, cour_in),
                (top_hbm, top_in),
                (mat_hbm, mat_in),
            ]
        )
    ]
    for load in loads:
        load.start()

    barrier = pltpu.get_barrier_semaphore()

    def greet_lev(d, _):
        pl.semaphore_signal(barrier, inc=1, device_id={"lev": lev_at(d)}, device_id_type=MESH)
        return _

    def greet_lat(d, _):
        pl.semaphore_signal(barrier, inc=1, device_id={"lat": lat_at(d)}, device_id_type=MESH)
        return _

    lax.fori_loop(1, n_lev, greet_lev, 0)
    lax.fori_loop(1, n_lat, greet_lat, 0)

    loads[0].wait()
    for t in range(2):
        for m in range(n_lev // 2):
            for kk in range(2):
                cols = pl.ds(m * 128, 128)
                a, b = pair(adj_in[t, kk, 0:8, cols], adj_in[t, kk, 8:16, cols])
                fwd_out[t, pl.ds(m * 32 + kk * 8, 8), :] = a
                fwd_out[t, pl.ds(m * 32 + 16 + kk * 8, 8), :] = b
    pl.semaphore_wait(barrier, n_lev + n_lat - 2)

    def block(i):
        return pl.ds(pl.multiple_of(i * 16, 16), 16)

    def fwd_copy(t, d):
        return pltpu.make_async_remote_copy(
            src_ref=fwd_out.at[t, block(lev_at(d)), :],
            dst_ref=fwd_in.at[t, block(lev), :],
            send_sem=fwd_send.at[t, d],
            recv_sem=fwd_recv.at[t, d],
            device_id={"lev": lev_at(d)},
            device_id_type=MESH,
        )

    def start_fwd(t):
        def step(d, _):
            fwd_copy(t, d).start()
            return _

        lax.fori_loop(1, n_lev, step, 0)

    start_fwd(0)
    start_fwd(1)
    for t in range(2):
        fwd_in[t, block(lev), :] = fwd_out[t, block(lev), :]

    for i in range(1, 6):
        loads[i].wait()
    owner, cell = owner_in[...], cell_in[...]
    valid = lanes((1, slots)) < count_in[...]
    owned = (lax.broadcasted_iota(I32, (n_lat, slots), 0) == owner) & valid
    upper = one_hot(lax.broadcasted_iota(I32, (slots, slots), 0) < lanes((slots, slots)))
    before = dot(one_hot(owned), upper)
    rank = jnp.sum(jnp.where(owned, before, 0.0), axis=0, keepdims=True).astype(I32)
    slot = jnp.where(valid, owner * HALF + rank, -1)
    row = cell // HALF
    packed = (row % TILES) * 128 + (row // TILES) * HALF + cell % HALF
    payload[...] = jnp.zeros((slots, 128), F32)
    payload[:, 0 : 2 * levels] = kern_in[...]
    payload[:, HALF : HALF + 2] = wt_in[...]
    turned = jnp.transpose(payload[...])
    small = turned[HALF : HALF + MSG, :]
    small = jnp.where(
        lax.broadcasted_iota(I32, (MSG, slots), 0) == 2, (packed + 1).astype(F32), small
    )
    table = jnp.concatenate([turned[0 : 2 * levels, :], small], axis=0)
    tall = 2 * levels + MSG
    table = jnp.concatenate(split(table), axis=0)

    def route(q, _):
        base = pl.multiple_of(q * 256, 256)
        spot = lax.broadcasted_iota(I32, (256, slots), 0) + base
        hits = one_hot(spot == slot)
        place[pl.ds(base, 256), :] = hits
        sent = dot(table, hits, (1, 1))
        sent = sent[:tall] + sent[tall:]
        for m in range(2):
            part = sent[:, m * 128 : (m + 1) * 128]
            a, b = pair(part[:levels], part[levels : 2 * levels])
            rest = part[2 * levels :]
            msg_out[q * 4 + m * 2, 0:levels, :] = a
            msg_out[q * 4 + m * 2 + 1, 0:levels, :] = b
            msg_out[q * 4 + m * 2, levels : levels + MSG, :] = rest
            msg_out[q * 4 + m * 2 + 1, levels : levels + MSG, :] = turn(rest, HALF)
        return _

    lax.fori_loop(0, n_lat // 4, route, 0)

    def msg_copy(d):
        return pltpu.make_async_remote_copy(
            src_ref=msg_out.at[lat_at(d)],
            dst_ref=msg_in.at[lat],
            send_sem=msg_send.at[d],
            recv_sem=msg_recv.at[d],
            device_id={"lat": lat_at(d)},
            device_id_type=MESH,
        )

    def start_msg(d, _):
        msg_copy(d).start()
        return _

    lax.fori_loop(1, n_lat, start_msg, 0)
    msg_in[lat] = msg_out[lat]

    loads[6].wait()
    for c in range(2):
        for p in range(TILES):
            a = cour_in[c, pl.ds(p, levels, stride=ROWS), :]
            b = cour_in[c, pl.ds(p + TILES, levels, stride=ROWS), :]
            cour_t[c, p] = jnp.concatenate([a, b], axis=1)
    c_lon_out[0], c_lon_out[1] = pack_lon([cour_t[0, p] for p in range(TILES)])
    c_lat_out[0], c_lat_out[1] = pack_lat([cour_t[1, p] for p in range(TILES)])

    def edge_copies(lon_out, lon_in, lat_out, lat_in, send, recv):
        copies = []
        for i, step in enumerate((-1, 1)):
            copies.append(
                pltpu.make_async_remote_copy(
                    src_ref=lon_out.at[i],
                    dst_ref=lon_in.at[i],
                    send_sem=send.at[i],
                    recv_sem=recv.at[i],
                    device_id={"lev": lev_at(step)},
                    device_id_type=MESH,
                )
            )
        for i, step in enumerate((-1, 1)):
            copies.append(
                pltpu.make_async_remote_copy(
                    src_ref=lat_out.at[i],
                    dst_ref=lat_in.at[i],
                    send_sem=send.at[2 + i],
                    recv_sem=recv.at[2 + i],
                    device_id={"lat": lat_at(step)},
                    device_id_type=MESH,
                )
            )
        return copies

    c_copies = edge_copies(c_lon_out, c_lon_in, c_lat_out, c_lat_in, c_send, c_recv)
    for copy in c_copies:
        copy.start()

    loads[7].wait()
    loads[8].wait()
    for g in range(mat_in.shape[0] // 2):
        wide = []
        for odd in range(2):
            high, low = split(jnp.transpose(mat_in[2 * g + odd]))
            wide += [high, high, low]
        mix[pl.ds(g * levels, levels), :] = jnp.concatenate(wide, axis=1)
    tops = jnp.concatenate([top_in[0:8, :], top_in[8:16, :]], axis=1)

    first, last = lat == 0, lat == n_lat - 1
    for copy in c_copies:
        copy.wait()
    from_east, from_west = c_lon_in[0], c_lon_in[1]
    from_north, from_south = c_lat_in[0], c_lat_in[1]
    from_north = jnp.where(last, 0.0, from_north)
    from_south = jnp.where(first, 0.0, from_south)
    rows_c = [cour_t[1, p] for p in range(TILES)]
    rows_c[0] = jnp.where(low_half(rows_c[0].shape) & first, 0.0, rows_c[0])
    rows_c = extend_lat(rows_c, from_south, from_north)
    for p in range(TILES):
        here = cour_t[0, p]
        before_x, after_x, after2_x = shift_lon(here, p, from_west, from_east, (-1, 1, 2))
        lon_w = face_weights(before_x, here, after_x, after2_x)
        lat_w = face_weights(rows_c[p + 1], rows_c[p + 2], rows_c[p + 3], rows_c[p + 4])
        weights[p, 0] = 1.0 + lon_w[2] + lat_w[2]
        for i, j in enumerate((0, 1, 3, 4)):
            weights[p, 1 + i] = lon_w[j]
            weights[p, 5 + i] = lat_w[j]

    def wait_msg(d, _):
        msg_copy(d).wait()
        return _

    lax.fori_loop(1, n_lat, wait_msg, 0)
    columns = TILES * 128

    def arrive(m, _):
        a, b = msg_in[2 * m], msg_in[2 * m + 1]
        one, two = pair(a[:levels], b[:levels])
        rest, _unused = pair(a[levels:], b[levels:])
        kern_rows[m, 0:levels, :] = one
        kern_rows[m, levels : 2 * levels, :] = two
        wk = jnp.concatenate([one * rest[0:1], two * rest[1:2]], axis=0)
        at = pl.ds(pl.multiple_of(m * 128, 128), 128)
        high, low = split(wk)
        weighted[0 : 2 * levels, at] = high
        weighted[2 * levels :, at] = low
        target = rest[2:3].astype(I32) - 1
        hot[:, at] = one_hot(lax.broadcasted_iota(I32, (columns, 128), 0) == target)
        return _

    lax.fori_loop(0, n_lat // 2, arrive, 0)
    for q in range(TILES // 2):
        got = dot(weighted[...], hot[pl.ds(q * 256, 256), :], (1, 1))
        got = got[: 2 * levels] + got[2 * levels :]
        for t in range(2):
            for i in range(2):
                deposit[t, 2 * q + i] = got[
                    t * levels : (t + 1) * levels, i * 128 : (i + 1) * 128
                ]

    def wait_fwd(t):
        def step(d, _):
            fwd_copy(t, d).wait()
            return _

        lax.fori_loop(1, n_lev, step, 0)

    for t in range(2):
        wait_fwd(t)
        for q in range(TILES // 2):
            x = jnp.concatenate(
                [
                    fwd_in[t, pl.ds(p, levels, stride=TILES), :] + deposit[t, p]
                    for p in (2 * q, 2 * q + 1)
                ],
                axis=1,
            )
            top = jnp.concatenate([tops[2 * q : 2 * q + 1], tops[2 * q + 1 : 2 * q + 2]], axis=1)
            stack = []
            for odd in range(2):
                high, low = split(jnp.where(top % 2 == odd, x, 0.0))
                stack += [high, low, high]
            mixed = dot(mix[...], jnp.concatenate(stack, axis=0))
            result = mixed[0:levels]
            for g in range(1, mat_in.shape[0] // 2):
                result = jnp.where(top // 2 == g, mixed[g * levels : (g + 1) * levels], result)
            high, low = split(result)
            conv_split[pl.ds(t * levels, levels), pl.ds(q * 256, 256)] = high
            conv_split[pl.ds((2 + t) * levels, levels), pl.ds(q * 256, 256)] = low
            conv[t, 2 * q] = result[:, :128]
            conv[t, 2 * q + 1] = result[:, 128:]
        tiles = [conv[t, p] for p in range(TILES)]
        rows_t = pl.ds(t * levels, levels)
        a_lon_out[0, rows_t, :], a_lon_out[1, rows_t, :] = pack_lon(tiles)
        a_lat_out[0, rows_t, :], a_lat_out[1, rows_t, :] = pack_lat(tiles)
    a_copies = edge_copies(a_lon_out, a_lon_in, a_lat_out, a_lat_in, a_send, a_recv)
    for copy in a_copies:
        copy.start()
    for copy in a_copies:
        copy.wait()

    def back_copy(t, d):
        return pltpu.make_async_remote_copy(
            src_ref=back_out.at[t, block(lev_at(d)), :],
            dst_ref=back_in.at[t, block(lev), :],
            send_sem=back_send.at[t, d],
            recv_sem=back_recv.at[t, d],
            device_id={"lev": lev_at(d)},
            device_id_type=MESH,
        )

    for t in range(2):
        rows_t = pl.ds(t * levels, levels)
        from_east, from_west = a_lon_in[0, rows_t, :], a_lon_in[1, rows_t, :]
        from_north, from_south = a_lat_in[0, rows_t, :], a_lat_in[1, rows_t, :]
        from_north = jnp.where(last, 0.0, from_north)
        from_south = jnp.where(first, 0.0, from_south)
        tiles = extend_lat([conv[t, p] for p in range(TILES)], from_south, from_north)
        for p in range(TILES):
            here = tiles[p + 2]
            around = shift_lon(here, p, from_west, from_east, (-2, -1, 1, 2))
            around += [tiles[p], tiles[p + 1], tiles[p + 3], tiles[p + 4]]
            total = weights[p, 0] * here
            for i in range(8):
                total = total + weights[p, 1 + i] * around[i]
            back_out[t, pl.ds(p, levels, stride=TILES), :] = total

        def start_back(d, _, t=t):
            back_copy(t, d).start()
            return _

        lax.fori_loop(1, n_lev, start_back, 0)
        back_in[t, block(lev), :] = back_out[t, block(lev), :]

    for m in range(n_lat // 4):
        picked = dot(conv_split[...], hot[:, pl.ds(m * 256, 256)])
        picked = picked[: 2 * levels] + picked[2 * levels :]
        for i in range(2):
            product = picked[:, i * 128 : (i + 1) * 128] * kern_rows[2 * m + i]
            sums = [
                jnp.sum(product[t * levels : (t + 1) * levels], axis=0, keepdims=True)
                for t in range(2)
            ]
            which = lax.broadcasted_iota(I32, (MSG, 128), 0)
            both = jnp.where(which == 0, sums[0], jnp.where(which == 1, sums[1], 0.0))
            ret_out[4 * m + 2 * i] = both
            ret_out[4 * m + 2 * i + 1] = turn(both, HALF)

    def ret_copy(d):
        return pltpu.make_async_remote_copy(
            src_ref=ret_out.at[lat_at(d)],
            dst_ref=ret_in.at[lat],
            send_sem=ret_send.at[d],
            recv_sem=ret_recv.at[d],
            device_id={"lat": lat_at(d)},
            device_id_type=MESH,
        )

    def start_ret(d, _):
        ret_copy(d).start()
        return _

    def wait_ret(d, _):
        ret_copy(d).wait()
        return _

    lax.fori_loop(1, n_lat, start_ret, 0)
    ret_in[lat] = ret_out[lat]
    lax.fori_loop(1, n_lat, wait_ret, 0)
    for m in range(n_lat // 2):
        both, _unused = pair(ret_in[2 * m], ret_in[2 * m + 1])
        ret_split[:, pl.ds(m * 128, 128)] = jnp.concatenate(split(both), axis=0)
    own = dot(ret_split[...], place[...])
    own = own[:MSG] + own[MSG:]
    sens_vm[...] = jnp.transpose(own)[:, 0:2]
    sens_store = pltpu.make_async_copy(sens_vm, sens_hbm, out_sem.at[0])
    sens_store.start()

    for t in range(2):

        def wait_back(d, _, t=t):
            back_copy(t, d).wait()
            return _

        lax.fori_loop(1, n_lev, wait_back, 0)
        for m in range(n_lev // 2):
            for kk in range(2):
                a, b = pair(
                    back_in[t, pl.ds(m * 32 + kk * 8, 8), :],
                    back_in[t, pl.ds(m * 32 + 16 + kk * 8, 8), :],
                )
                out_vm[t, kk, 0:8, pl.ds(m * 128, 128)] = a
                out_vm[t, kk, 8:16, pl.ds(m * 128, 128)] = b
    out_store = pltpu.make_async_copy(out_vm, out_hbm, out_sem.at[1])
    out_store.start()
    out_store.wait()
    sens_store.wait()


def per_device(
    n_lev,
    n_lat,
    adjoint_in,
    courant,
    cloud_top,
    conv_inverse,
    sounding_kernel,
    sounding_weight,
    sounding_owner,
    sounding_cell,
    sounding_count,
):
    levels = 2 * n_lev
    slots = sounding_kernel.shape[2]
    classes = conv_inverse.shape[0]
    columns = TILES * 128
    spots = n_lat * HALF
    operands = (
        adjoint_in,
        courant.reshape(2, levels * ROWS, HALF),
        cloud_top,
        conv_inverse,
        sounding_kernel.reshape(slots, 2 * levels),
        sounding_weight.reshape(slots, 2),
        sounding_owner.reshape(1, slots),
        sounding_cell.reshape(1, slots),
        sounding_count,
    )
    vm, dma = pltpu.VMEM, pltpu.SemaphoreType.DMA
    scratch = [vm(x.shape, x.dtype) for x in operands]
    scratch += [
        vm(adjoint_in.shape, F32),
        vm((slots, 2), F32),
    ]
    scratch += [vm((2, n_lev * 16, 128), F32) for _ in range(4)]
    scratch += [vm((n_lat, levels + MSG, 128), F32) for _ in range(2)]
    scratch += [vm((n_lat, MSG, 128), F32) for _ in range(2)]
    scratch += [vm((2, levels, 128), F32) for _ in range(4)]
    scratch += [vm((2, 2 * levels, 128), F32) for _ in range(4)]
    scratch += [
        vm((spots, slots), BF16),
        vm((slots, 128), F32),
        vm((n_lat // 2, 2 * levels, 128), F32),
        vm((4 * levels, spots), BF16),
        vm((columns, spots), BF16),
        vm((2, TILES, levels, 128), F32),
        vm((2, TILES, levels, 128), F32),
        vm((TILES, 9, levels, 128), F32),
        vm((classes // 2 * levels, 6 * levels), BF16),
        vm((2, TILES, levels, 128), F32),
        vm((4 * levels, columns), BF16),
        vm((2 * MSG, spots), BF16),
        dma((9,)),
        dma((2,)),
    ]
    scratch += [dma((2, n_lev)) for _ in range(4)]
    scratch += [dma((n_lat,)) for _ in range(4)]
    scratch += [dma((4,)) for _ in range(4)]
    any_space = pl.BlockSpec(memory_space=pl.ANY)
    out, sens = pl.pallas_call(
        functools.partial(kernel, n_lev, n_lat),
        out_shape=(
            jax.ShapeDtypeStruct(adjoint_in.shape, F32),
            jax.ShapeDtypeStruct((slots, 2), F32),
        ),
        in_specs=[any_space] * len(operands),
        out_specs=(any_space, any_space),
        scratch_shapes=scratch,
        compiler_params=pltpu.CompilerParams(
            collective_id=0, has_side_effects=True, vmem_limit_bytes=40 * 2**20
        ),
    )(*operands)
    return out, sens.reshape(1, 1, slots, 2)


def solution(mesh):
    placed = (
        P(None, "lev", "lat", None),
        P(None, None, "lat", "lev"),
        P("lat", "lev"),
        P(),
        P("lev", "lat", None, None),
        P("lev", "lat", None, None),
        P("lev", "lat", None),
        P("lev", "lat", None),
        P("lev", "lat"),
    )
    return jax.shard_map(
        functools.partial(per_device, mesh.shape["lev"], mesh.shape["lat"]),
        mesh=mesh,
        in_specs=placed,
        out_specs=(P(None, "lev", "lat", None), P("lev", "lat", None, None)),
        check_vma=False,
    )
```

```python
import functools

import jax
import jax.numpy as jnp
from jax import lax
from jax.experimental import pallas as pl
from jax.experimental.pallas import tpu as pltpu
from jax.sharding import PartitionSpec as P

MESH = pl.DeviceIdType.MESH
F32, BF16, I32 = jnp.float32, jnp.bfloat16, jnp.int32
ROWS = 16
TILES = 8
HALF = 64
MSG = 8


def lanes(shape):
    return lax.broadcasted_iota(I32, shape, len(shape) - 1)


def turn(x, shift):
    shift = shift % 128
    return x if shift == 0 else pltpu.roll(x, shift, x.ndim - 1)


def low_half(shape):
    return lanes(shape) < HALF


def pair(a, b):
    low = low_half(a.shape)
    return jnp.where(low, a, turn(b, HALF)), jnp.where(low, turn(a, HALF), b)


def split(x):
    high = x.astype(BF16)
    return high, (x - high.astype(F32)).astype(BF16)


def dot(a, b, contract=(1, 0)):
    return lax.dot_general(
        a, b, (((contract[0],), (contract[1],)), ((), ())), preferred_element_type=F32
    )


def one_hot(mask):
    return jnp.where(mask, 1.0, 0.0).astype(BF16)


def pack_lon(tiles):
    x = lanes(tiles[0].shape) % HALF
    to_west, to_east = tiles[0], turn(tiles[0], 66)
    for p in range(1, TILES):
        here = x // 2 == p
        to_west = jnp.where(here, turn(tiles[p], 2 * p), to_west)
        to_east = jnp.where(here, turn(tiles[p], 2 * p + 66), to_east)
    return to_west, to_east


def shift_lon(tile, p, from_west, from_east, steps):
    x = lanes(tile.shape) % HALF
    east = turn(from_east, HALF - 2 * p)
    west = turn(from_west, 126 - 2 * p)
    out = []
    for d in steps:
        if d > 0:
            out.append(turn(jnp.where(x < d, east, tile), -d))
        else:
            out.append(turn(jnp.where(x >= HALF + d, west, tile), -d))
    return out


def pack_lat(tiles):
    low = low_half(tiles[0].shape)
    to_south = jnp.where(low, tiles[0], turn(tiles[1], HALF))
    to_north = jnp.where(low, turn(tiles[6], HALF), tiles[7])
    return to_south, to_north


def extend_lat(tiles, from_south, from_north):
    low = low_half(tiles[0].shape)
    return (
        [
            jnp.where(low, from_south, turn(tiles[6], HALF)),
            turn(jnp.where(low, tiles[7], from_south), HALF),
        ]
        + list(tiles)
        + [
            turn(jnp.where(low, from_north, tiles[0]), HALF),
            jnp.where(low, turn(tiles[1], HALF), from_north),
        ]
    )


def face_weights(before, here, after, after2):
    def parts(c):
        pos, neg = jnp.maximum(c, 0.0), jnp.minimum(c, 0.0)
        return pos, neg, 0.25 * pos * (1.0 - pos), 0.25 * neg * (1.0 + neg)

    _, _, _, sn_before = parts(before)
    _, neg_here, sp_here, _ = parts(here)
    pos_after, _, _, sn_after = parts(after)
    _, _, sp_after2, _ = parts(after2)
    own = neg_here + sp_here
    nxt = pos_after + sn_after
    return sn_before, -own - sn_before, own - nxt, nxt + sp_after2, -sp_after2


def kernel(
    n_lev,
    n_lat,
    adj_hbm,
    cour_hbm,
    top_hbm,
    mat_hbm,
    kern_hbm,
    wt_hbm,
    owner_hbm,
    cell_hbm,
    count_hbm,
    out_ref,
    sens_ref,
    adj_in,
    cour_in,
    top_in,
    mat_in,
    kern_in,
    wt_in,
    owner_in,
    cell_in,
    count_in,
    fwd_out,
    fwd_in,
    back_out,
    back_in,
    msg_out,
    msg_in,
    ret_out,
    ret_in,
    c_lon_out,
    c_lon_in,
    c_lat_out,
    c_lat_in,
    a_lon_out,
    a_lon_in,
    a_lat_out,
    a_lat_in,
    place,
    kern_rows,
    weighted,
    hot,
    deposit,
    cour_t,
    weights,
    mix,
    conv,
    conv_split,
    ret_split,
    in_sem,
    fwd_send,
    fwd_recv,
    back_send,
    back_recv,
    msg_send,
    msg_recv,
    ret_send,
    ret_recv,
    c_send,
    c_recv,
    a_send,
    a_recv,
):
    lev, lat = lax.axis_index("lev"), lax.axis_index("lat")
    levels = 2 * n_lev
    slots = owner_in.shape[1]

    def lev_at(d):
        return lax.rem(lev + d + n_lev, n_lev)

    def lat_at(d):
        return lax.rem(lat + d + n_lat, n_lat)

    loads = [
        pltpu.make_async_copy(source, target, in_sem.at[i])
        for i, (source, target) in enumerate(
            [
                (adj_hbm, adj_in),
                (owner_hbm, owner_in),
                (cell_hbm, cell_in),
                (count_hbm, count_in),
                (kern_hbm, kern_in),
                (wt_hbm, wt_in),
                (cour_hbm, cour_in),
                (top_hbm, top_in),
                (mat_hbm, mat_in),
            ]
        )
    ]
    for load in loads:
        load.start()

    barrier = pltpu.get_barrier_semaphore()

    def greet_lev(d, _):
        pl.semaphore_signal(barrier, inc=1, device_id={"lev": lev_at(d)}, device_id_type=MESH)
        return _

    def greet_lat(d, _):
        pl.semaphore_signal(barrier, inc=1, device_id={"lat": lat_at(d)}, device_id_type=MESH)
        return _

    lax.fori_loop(1, n_lev, greet_lev, 0)
    lax.fori_loop(1, n_lat, greet_lat, 0)

    loads[0].wait()
    for t in range(2):
        for m in range(n_lev // 2):
            for kk in range(2):
                cols = pl.ds(m * 128, 128)
                a, b = pair(adj_in[t, kk, 0:8, cols], adj_in[t, kk, 8:16, cols])
                fwd_out[t, pl.ds(m * 32 + kk * 8, 8), :] = a
                fwd_out[t, pl.ds(m * 32 + 16 + kk * 8, 8), :] = b
    pl.semaphore_wait(barrier, n_lev + n_lat - 2)


    def block(i):
        return pl.ds(pl.multiple_of(i * 16, 16), 16)

    def fwd_copy(t, d):
        return pltpu.make_async_remote_copy(
            src_ref=fwd_out.at[t, block(lev_at(d)), :],
            dst_ref=fwd_in.at[t, block(lev), :],
            send_sem=fwd_send.at[t, d],
            recv_sem=fwd_recv.at[t, d],
            device_id={"lev": lev_at(d)},
            device_id_type=MESH,
        )

    def start_fwd(t):
        def step(d, _):
            fwd_copy(t, d).start()
            return _

        lax.fori_loop(1, n_lev, step, 0)

    start_fwd(0)
    start_fwd(1)
    for t in range(2):
        fwd_in[t, block(lev), :] = fwd_out[t, block(lev), :]


    for i in range(1, 6):
        loads[i].wait()
    owner, cell = owner_in[...], cell_in[...]
    valid = lanes((1, slots)) < count_in[...]
    owned = (lax.broadcasted_iota(I32, (n_lat, slots), 0) == owner) & valid
    upper = one_hot(lax.broadcasted_iota(I32, (slots, slots), 0) < lanes((slots, slots)))
    before = dot(one_hot(owned), upper)
    rank = jnp.sum(jnp.where(owned, before, 0.0), axis=0, keepdims=True).astype(I32)
    slot = jnp.where(valid, owner * HALF + rank, -1)
    row = cell // HALF
    packed = (row % TILES) * 128 + (row // TILES) * HALF + cell % HALF
    which = lax.broadcasted_iota(I32, (MSG, slots), 0)
    small = jnp.where(which == 2, (packed + 1).astype(F32), 0.0)
    for t in range(2):
        small = jnp.where(which == t, wt_in[t : t + 1, :], small)
    table = jnp.concatenate([kern_in[...], small], axis=0)
    tall = 2 * levels + MSG
    table = jnp.concatenate(split(table), axis=0)

    def route(q, _):
        base = pl.multiple_of(q * 256, 256)
        spot = lax.broadcasted_iota(I32, (256, slots), 0) + base
        hits = one_hot(spot == slot)
        place[pl.ds(base, 256), :] = hits
        sent = dot(table, hits, (1, 1))
        sent = sent[:tall] + sent[tall:]
        for m in range(2):
            part = sent[:, m * 128 : (m + 1) * 128]
            a, b = pair(part[:levels], part[levels : 2 * levels])
            rest = part[2 * levels :]
            msg_out[q * 4 + m * 2, 0:levels, :] = a
            msg_out[q * 4 + m * 2 + 1, 0:levels, :] = b
            msg_out[q * 4 + m * 2, levels : levels + MSG, :] = rest
            msg_out[q * 4 + m * 2 + 1, levels : levels + MSG, :] = turn(rest, HALF)
        return _

    lax.fori_loop(0, n_lat // 4, route, 0)

    def msg_copy(d):
        return pltpu.make_async_remote_copy(
            src_ref=msg_out.at[lat_at(d)],
            dst_ref=msg_in.at[lat],
            send_sem=msg_send.at[d],
            recv_sem=msg_recv.at[d],
            device_id={"lat": lat_at(d)},
            device_id_type=MESH,
        )

    def start_msg(d, _):
        msg_copy(d).start()
        return _


    lax.fori_loop(1, n_lat, start_msg, 0)
    msg_in[lat] = msg_out[lat]


    loads[6].wait()
    for c in range(2):
        for p in range(TILES):
            a = cour_in[c, pl.ds(p, levels, stride=ROWS), :]
            b = cour_in[c, pl.ds(p + TILES, levels, stride=ROWS), :]
            cour_t[c, p] = jnp.concatenate([a, b], axis=1)
    c_lon_out[0], c_lon_out[1] = pack_lon([cour_t[0, p] for p in range(TILES)])
    c_lat_out[0], c_lat_out[1] = pack_lat([cour_t[1, p] for p in range(TILES)])

    def edge_copies(lon_out, lon_in, lat_out, lat_in, send, recv):
        copies = []
        for i, step in enumerate((-1, 1)):
            copies.append(
                pltpu.make_async_remote_copy(
                    src_ref=lon_out.at[i],
                    dst_ref=lon_in.at[i],
                    send_sem=send.at[i],
                    recv_sem=recv.at[i],
                    device_id={"lev": lev_at(step)},
                    device_id_type=MESH,
                )
            )
        for i, step in enumerate((-1, 1)):
            copies.append(
                pltpu.make_async_remote_copy(
                    src_ref=lat_out.at[i],
                    dst_ref=lat_in.at[i],
                    send_sem=send.at[2 + i],
                    recv_sem=recv.at[2 + i],
                    device_id={"lat": lat_at(step)},
                    device_id_type=MESH,
                )
            )
        return copies

    c_copies = edge_copies(c_lon_out, c_lon_in, c_lat_out, c_lat_in, c_send, c_recv)
    for copy in c_copies:
        copy.start()


    loads[7].wait()
    loads[8].wait()
    for g in range(mat_in.shape[0] // 2):
        wide = []
        for odd in range(2):
            high, low = split(jnp.transpose(mat_in[2 * g + odd]))
            wide += [high, high, low]
        mix[pl.ds(g * levels, levels), :] = jnp.concatenate(wide, axis=1)
    tops = jnp.concatenate([top_in[0:8, :], top_in[8:16, :]], axis=1)

    first, last = lat == 0, lat == n_lat - 1
    for copy in c_copies:
        copy.wait()
    from_east, from_west = c_lon_in[0], c_lon_in[1]
    from_north, from_south = c_lat_in[0], c_lat_in[1]
    from_north = jnp.where(last, 0.0, from_north)
    from_south = jnp.where(first, 0.0, from_south)
    rows_c = [cour_t[1, p] for p in range(TILES)]
    rows_c[0] = jnp.where(low_half(rows_c[0].shape) & first, 0.0, rows_c[0])
    rows_c = extend_lat(rows_c, from_south, from_north)
    for p in range(TILES):
        here = cour_t[0, p]
        before_x, after_x, after2_x = shift_lon(here, p, from_west, from_east, (-1, 1, 2))
        lon_w = face_weights(before_x, here, after_x, after2_x)
        lat_w = face_weights(rows_c[p + 1], rows_c[p + 2], rows_c[p + 3], rows_c[p + 4])
        weights[p, 0] = 1.0 + lon_w[2] + lat_w[2]
        for i, j in enumerate((0, 1, 3, 4)):
            weights[p, 1 + i] = lon_w[j]
            weights[p, 5 + i] = lat_w[j]


    def wait_msg(d, _):
        msg_copy(d).wait()
        return _

    lax.fori_loop(1, n_lat, wait_msg, 0)

    columns = TILES * 128

    def arrive(m, _):
        a, b = msg_in[2 * m], msg_in[2 * m + 1]
        one, two = pair(a[:levels], b[:levels])
        rest, _unused = pair(a[levels:], b[levels:])
        kern_rows[m, 0:levels, :] = one
        kern_rows[m, levels : 2 * levels, :] = two
        wk = jnp.concatenate([one * rest[0:1], two * rest[1:2]], axis=0)
        at = pl.ds(pl.multiple_of(m * 128, 128), 128)
        high, low = split(wk)
        weighted[0 : 2 * levels, at] = high
        weighted[2 * levels :, at] = low
        target = rest[2:3].astype(I32) - 1
        hot[:, at] = one_hot(lax.broadcasted_iota(I32, (columns, 128), 0) == target)
        return _

    lax.fori_loop(0, n_lat // 2, arrive, 0)
    for q in range(TILES // 2):
        got = dot(weighted[...], hot[pl.ds(q * 256, 256), :], (1, 1))
        got = got[: 2 * levels] + got[2 * levels :]
        for t in range(2):
            for i in range(2):
                deposit[t, 2 * q + i] = got[
                    t * levels : (t + 1) * levels, i * 128 : (i + 1) * 128
                ]


    def wait_fwd(t):
        def step(d, _):
            fwd_copy(t, d).wait()
            return _

        lax.fori_loop(1, n_lev, step, 0)

    a_copies = []
    for t in range(2):
        wait_fwd(t)
        for q in range(TILES // 2):
            x = jnp.concatenate(
                [
                    fwd_in[t, pl.ds(p, levels, stride=TILES), :] + deposit[t, p]
                    for p in (2 * q, 2 * q + 1)
                ],
                axis=1,
            )
            top = jnp.concatenate([tops[2 * q : 2 * q + 1], tops[2 * q + 1 : 2 * q + 2]], axis=1)
            stack = []
            for odd in range(2):
                high, low = split(jnp.where(top % 2 == odd, x, 0.0))
                stack += [high, low, high]
            mixed = dot(mix[...], jnp.concatenate(stack, axis=0))
            result = mixed[0:levels]
            for g in range(1, mat_in.shape[0] // 2):
                result = jnp.where(top // 2 == g, mixed[g * levels : (g + 1) * levels], result)
            high, low = split(result)
            conv_split[pl.ds(t * levels, levels), pl.ds(q * 256, 256)] = high
            conv_split[pl.ds((2 + t) * levels, levels), pl.ds(q * 256, 256)] = low
            conv[t, 2 * q] = result[:, :128]
            conv[t, 2 * q + 1] = result[:, 128:]
        tiles = [conv[t, p] for p in range(TILES)]
        a_lon_out[t, 0], a_lon_out[t, 1] = pack_lon(tiles)
        a_lat_out[t, 0], a_lat_out[t, 1] = pack_lat(tiles)
        a_copies.append(
            edge_copies(
                a_lon_out.at[t],
                a_lon_in.at[t],
                a_lat_out.at[t],
                a_lat_in.at[t],
                a_send.at[t],
                a_recv.at[t],
            )
        )
        for copy in a_copies[t]:
            copy.start()


    def back_copy(t, d):
        return pltpu.make_async_remote_copy(
            src_ref=back_out.at[t, block(lev_at(d)), :],
            dst_ref=back_in.at[t, block(lev), :],
            send_sem=back_send.at[t, d],
            recv_sem=back_recv.at[t, d],
            device_id={"lev": lev_at(d)},
            device_id_type=MESH,
        )

    for t in range(2):
        for copy in a_copies[t]:
            copy.wait()
        from_east, from_west = a_lon_in[t, 0], a_lon_in[t, 1]
        from_north, from_south = a_lat_in[t, 0], a_lat_in[t, 1]
        from_north = jnp.where(last, 0.0, from_north)
        from_south = jnp.where(first, 0.0, from_south)
        tiles = extend_lat([conv[t, p] for p in range(TILES)], from_south, from_north)
        for p in range(TILES):
            here = tiles[p + 2]
            around = shift_lon(here, p, from_west, from_east, (-2, -1, 1, 2))
            around += [tiles[p], tiles[p + 1], tiles[p + 3], tiles[p + 4]]
            total = weights[p, 0] * here
            for i in range(8):
                total = total + weights[p, 1 + i] * around[i]
            back_out[t, pl.ds(p, levels, stride=TILES), :] = total

        def start_back(d, _, t=t):
            back_copy(t, d).start()
            return _

        lax.fori_loop(1, n_lev, start_back, 0)
        back_in[t, block(lev), :] = back_out[t, block(lev), :]


    for m in range(n_lat // 4):
        picked = dot(conv_split[...], hot[:, pl.ds(m * 256, 256)])
        picked = picked[: 2 * levels] + picked[2 * levels :]
        for i in range(2):
            product = picked[:, i * 128 : (i + 1) * 128] * kern_rows[2 * m + i]
            sums = [
                jnp.sum(product[t * levels : (t + 1) * levels], axis=0, keepdims=True)
                for t in range(2)
            ]
            which = lax.broadcasted_iota(I32, (MSG, 128), 0)
            both = jnp.where(which == 0, sums[0], jnp.where(which == 1, sums[1], 0.0))
            ret_out[4 * m + 2 * i] = both
            ret_out[4 * m + 2 * i + 1] = turn(both, HALF)

    def ret_copy(d):
        return pltpu.make_async_remote_copy(
            src_ref=ret_out.at[lat_at(d)],
            dst_ref=ret_in.at[lat],
            send_sem=ret_send.at[d],
            recv_sem=ret_recv.at[d],
            device_id={"lat": lat_at(d)},
            device_id_type=MESH,
        )

    def start_ret(d, _):
        ret_copy(d).start()
        return _

    def wait_ret(d, _):
        ret_copy(d).wait()
        return _


    lax.fori_loop(1, n_lat, start_ret, 0)
    ret_in[lat] = ret_out[lat]
    lax.fori_loop(1, n_lat, wait_ret, 0)

    for m in range(n_lat // 2):
        both, _unused = pair(ret_in[2 * m], ret_in[2 * m + 1])
        ret_split[:, pl.ds(m * 128, 128)] = jnp.concatenate(split(both), axis=0)
    own = dot(ret_split[...], place[...])
    own = own[:MSG] + own[MSG:]
    sens_ref[...] = own[0:2]


    for t in range(2):

        def wait_back(d, _, t=t):
            back_copy(t, d).wait()
            return _

        lax.fori_loop(1, n_lev, wait_back, 0)
        for m in range(n_lev // 2):
            for kk in range(2):
                a, b = pair(
                    back_in[t, pl.ds(m * 32 + kk * 8, 8), :],
                    back_in[t, pl.ds(m * 32 + 16 + kk * 8, 8), :],
                )
                out_ref[t, kk, 0:8, pl.ds(m * 128, 128)] = a
                out_ref[t, kk, 8:16, pl.ds(m * 128, 128)] = b


def per_device(
    n_lev,
    n_lat,
    adjoint_in,
    courant,
    cloud_top,
    conv_inverse,
    sounding_kernel,
    sounding_weight,
    sounding_owner,
    sounding_cell,
    sounding_count,
):
    levels = 2 * n_lev
    slots = sounding_kernel.shape[2]
    classes = conv_inverse.shape[0]
    columns = TILES * 128
    spots = n_lat * HALF
    operands = (
        adjoint_in,
        courant.reshape(2, levels * ROWS, HALF),
        cloud_top,
        conv_inverse,
        sounding_kernel.reshape(slots, 2 * levels).T,
        sounding_weight.reshape(slots, 2).T,
        sounding_owner.reshape(1, slots),
        sounding_cell.reshape(1, slots),
        sounding_count,
    )
    vm, dma = pltpu.VMEM, pltpu.SemaphoreType.DMA
    scratch = [vm(x.shape, x.dtype) for x in operands]
    scratch += [vm((2, n_lev * 16, 128), F32) for _ in range(4)]
    scratch += [vm((n_lat, levels + MSG, 128), F32) for _ in range(2)]
    scratch += [vm((n_lat, MSG, 128), F32) for _ in range(2)]
    scratch += [vm((2, levels, 128), F32) for _ in range(4)]
    scratch += [vm((2, 2, levels, 128), F32) for _ in range(4)]
    scratch += [
        vm((spots, slots), BF16),
        vm((n_lat // 2, 2 * levels, 128), F32),
        vm((4 * levels, spots), BF16),
        vm((columns, spots), BF16),
        vm((2, TILES, levels, 128), F32),
        vm((2, TILES, levels, 128), F32),
        vm((TILES, 9, levels, 128), F32),
        vm((classes // 2 * levels, 6 * levels), BF16),
        vm((2, TILES, levels, 128), F32),
        vm((4 * levels, columns), BF16),
        vm((2 * MSG, spots), BF16),
        dma((9,)),
    ]
    scratch += [dma((2, n_lev)) for _ in range(4)]
    scratch += [dma((n_lat,)) for _ in range(4)]
    scratch += [dma((4,)) for _ in range(2)]
    scratch += [dma((2, 4)) for _ in range(2)]
    in_hbm = pl.BlockSpec(memory_space=pltpu.HBM)
    in_vmem = pl.BlockSpec(memory_space=pltpu.VMEM)
    out, sens = pl.pallas_call(
        functools.partial(kernel, n_lev, n_lat),
        out_shape=(
            jax.ShapeDtypeStruct(adjoint_in.shape, F32),
            jax.ShapeDtypeStruct((2, slots), F32),
        ),
        in_specs=[in_hbm] * len(operands),
        out_specs=(in_vmem, in_vmem),
        scratch_shapes=scratch,
        compiler_params=pltpu.CompilerParams(
            collective_id=0, has_side_effects=True, vmem_limit_bytes=40 * 2**20
        ),
    )(*operands)
    return out, sens.T.reshape(1, 1, slots, 2)


def solution(mesh):
    placed = (
        P(None, "lev", "lat", None),
        P(None, None, "lat", "lev"),
        P("lat", "lev"),
        P(),
        P("lev", "lat", None, None),
        P("lev", "lat", None, None),
        P("lev", "lat", None),
        P("lev", "lat", None),
        P("lev", "lat"),
    )
    return jax.shard_map(
        functools.partial(per_device, mesh.shape["lev"], mesh.shape["lat"]),
        mesh=mesh,
        in_specs=placed,
        out_specs=(P(None, "lev", "lat", None), P("lev", "lat", None, None)),
        check_vma=False,
    )
```

```python
import functools

import jax
import jax.numpy as jnp
from jax import lax
from jax.experimental import pallas as pl
from jax.experimental.pallas import tpu as pltpu
from jax.sharding import PartitionSpec as P

MESH = pl.DeviceIdType.MESH
F32, BF16, I32 = jnp.float32, jnp.bfloat16, jnp.int32
ROWS = 16
TILES = 8
HALF = 64
MSG = 8


def lanes(shape):
    return lax.broadcasted_iota(I32, shape, len(shape) - 1)


def turn(x, shift):
    shift = shift % 128
    return x if shift == 0 else pltpu.roll(x, shift, x.ndim - 1)


def low_half(shape):
    return lanes(shape) < HALF


def pair(a, b):
    low = low_half(a.shape)
    return jnp.where(low, a, turn(b, HALF)), jnp.where(low, turn(a, HALF), b)


def split(x):
    high = x.astype(BF16)
    return high, (x - high.astype(F32)).astype(BF16)


def dot(a, b, contract=(1, 0)):
    return lax.dot_general(
        a, b, (((contract[0],), (contract[1],)), ((), ())), preferred_element_type=F32
    )


def one_hot(mask):
    return jnp.where(mask, 1.0, 0.0).astype(BF16)


def pack_lon(tiles):
    x = lanes(tiles[0].shape) % HALF
    to_west, to_east = tiles[0], turn(tiles[0], 66)
    for p in range(1, TILES):
        here = x // 2 == p
        to_west = jnp.where(here, turn(tiles[p], 2 * p), to_west)
        to_east = jnp.where(here, turn(tiles[p], 2 * p + 66), to_east)
    return to_west, to_east


def shift_lon(tile, p, from_west, from_east, steps):
    x = lanes(tile.shape) % HALF
    east = turn(from_east, HALF - 2 * p)
    west = turn(from_west, 126 - 2 * p)
    out = []
    for d in steps:
        if d > 0:
            out.append(turn(jnp.where(x < d, east, tile), -d))
        else:
            out.append(turn(jnp.where(x >= HALF + d, west, tile), -d))
    return out


def pack_lat(tiles):
    low = low_half(tiles[0].shape)
    to_south = jnp.where(low, tiles[0], turn(tiles[1], HALF))
    to_north = jnp.where(low, turn(tiles[6], HALF), tiles[7])
    return to_south, to_north


def extend_lat(tiles, from_south, from_north):
    low = low_half(tiles[0].shape)
    return (
        [
            jnp.where(low, from_south, turn(tiles[6], HALF)),
            turn(jnp.where(low, tiles[7], from_south), HALF),
        ]
        + list(tiles)
        + [
            turn(jnp.where(low, from_north, tiles[0]), HALF),
            jnp.where(low, turn(tiles[1], HALF), from_north),
        ]
    )


def face_weights(before, here, after, after2):
    def parts(c):
        pos, neg = jnp.maximum(c, 0.0), jnp.minimum(c, 0.0)
        return pos, neg, 0.25 * pos * (1.0 - pos), 0.25 * neg * (1.0 + neg)

    _, _, _, sn_before = parts(before)
    _, neg_here, sp_here, _ = parts(here)
    pos_after, _, _, sn_after = parts(after)
    _, _, sp_after2, _ = parts(after2)
    own = neg_here + sp_here
    nxt = pos_after + sn_after
    return sn_before, -own - sn_before, own - nxt, nxt + sp_after2, -sp_after2


def kernel(
    n_lev,
    n_lat,
    adj_hbm,
    cour_hbm,
    top_hbm,
    mat_hbm,
    kern_hbm,
    wt_hbm,
    owner_hbm,
    cell_hbm,
    count_hbm,
    out_ref,
    sens_ref,
    adj_in,
    cour_in,
    top_in,
    mat_in,
    kern_in,
    wt_in,
    owner_in,
    cell_in,
    count_in,
    fwd_out,
    fwd_in,
    back_out,
    back_in,
    msg_out,
    msg_in,
    ret_out,
    ret_in,
    c_lon_out,
    c_lon_in,
    c_lat_out,
    c_lat_in,
    a_lon_out,
    a_lon_in,
    a_lat_out,
    a_lat_in,
    place,
    kern_rows,
    weighted,
    hot,
    deposit,
    cour_t,
    weights,
    mix,
    conv,
    conv_split,
    ret_split,
    in_sem,
    fwd_send,
    fwd_recv,
    back_send,
    back_recv,
    msg_send,
    msg_recv,
    ret_send,
    ret_recv,
    c_send,
    c_recv,
    a_send,
    a_recv,
):
    lev, lat = lax.axis_index("lev"), lax.axis_index("lat")
    levels = 2 * n_lev
    slots = owner_in.shape[1]

    def lev_at(d):
        return lax.rem(lev + d + n_lev, n_lev)

    def lat_at(d):
        return lax.rem(lat + d + n_lat, n_lat)

    n_y = max(2, n_lat // 8)
    n_x = n_lat // (2 * n_y)
    at_x, at_y, core = lat // (2 * n_y), lax.rem(lat // 2, n_y), lax.rem(lat, 2)

    def hops(step):
        return min(step[0], n_x - step[0]) + min(step[1], n_y - step[1])

    chips = sorted(((i, j) for i in range(n_x) for j in range(n_y)), key=hops, reverse=True)

    def chip_at(n, sign):
        i, j = chips[n]
        return lax.rem(at_x + sign * i + n_x, n_x) * n_y + lax.rem(at_y + sign * j + n_y, n_y)

    def far(i):
        half = (i + 1) // 2
        return n_lev // 2 + half * (1 - 2 * lax.rem(i, 2))

    loads = [
        pltpu.make_async_copy(source, target, in_sem.at[i])
        for i, (source, target) in enumerate(
            [
                (adj_hbm, adj_in),
                (owner_hbm, owner_in),
                (cell_hbm, cell_in),
                (count_hbm, count_in),
                (kern_hbm, kern_in),
                (wt_hbm, wt_in),
                (cour_hbm, cour_in),
                (top_hbm, top_in),
                (mat_hbm, mat_in),
            ]
        )
    ]
    for load in loads:
        load.start()

    barrier = pltpu.get_barrier_semaphore()

    def greet_lev(d, _):
        pl.semaphore_signal(barrier, inc=1, device_id={"lev": lev_at(d)}, device_id_type=MESH)
        return _

    def greet_lat(d, _):
        pl.semaphore_signal(barrier, inc=1, device_id={"lat": lat_at(d)}, device_id_type=MESH)
        return _

    lax.fori_loop(1, n_lev, greet_lev, 0)
    lax.fori_loop(1, n_lat, greet_lat, 0)

    loads[0].wait()
    for t in range(2):
        for m in range(n_lev // 2):
            for kk in range(2):
                cols = pl.ds(m * 128, 128)
                a, b = pair(adj_in[t, kk, 0:8, cols], adj_in[t, kk, 8:16, cols])
                fwd_out[t, pl.ds(m * 32 + kk * 8, 8), :] = a
                fwd_out[t, pl.ds(m * 32 + 16 + kk * 8, 8), :] = b
    pl.semaphore_wait(barrier, n_lev + n_lat - 2)


    def block(i):
        return pl.ds(pl.multiple_of(i * 16, 16), 16)

    def fwd_copy(t, d):
        return pltpu.make_async_remote_copy(
            src_ref=fwd_out.at[t, block(lev_at(d)), :],
            dst_ref=fwd_in.at[t, block(lev), :],
            send_sem=fwd_send.at[t, d],
            recv_sem=fwd_recv.at[t, d],
            device_id={"lev": lev_at(d)},
            device_id_type=MESH,
        )

    def start_fwd(t):
        def step(i, _):
            fwd_copy(t, far(i)).start()
            return _

        lax.fori_loop(0, n_lev - 1, step, 0)

    start_fwd(0)
    start_fwd(1)
    for t in range(2):
        fwd_in[t, block(lev), :] = fwd_out[t, block(lev), :]


    for i in range(1, 6):
        loads[i].wait()
    owner, cell = owner_in[...], cell_in[...]
    valid = lanes((1, slots)) < count_in[...]
    owned = (lax.broadcasted_iota(I32, (n_lat, slots), 0) == owner) & valid
    upper = one_hot(lax.broadcasted_iota(I32, (slots, slots), 0) < lanes((slots, slots)))
    before = dot(one_hot(owned), upper)
    rank = jnp.sum(jnp.where(owned, before, 0.0), axis=0, keepdims=True).astype(I32)
    slot = jnp.where(valid, owner * HALF + rank, -1)
    row = cell // HALF
    packed = (row % TILES) * 128 + (row // TILES) * HALF + cell % HALF
    which = lax.broadcasted_iota(I32, (MSG, slots), 0)
    small = jnp.where(which == 2, (packed + 1).astype(F32), 0.0)
    for t in range(2):
        small = jnp.where(which == t, wt_in[t : t + 1, :], small)
    table = jnp.concatenate([kern_in[...], small], axis=0)
    tall = 2 * levels + MSG
    table = jnp.concatenate(split(table), axis=0)

    def route(m):
        base = pl.multiple_of(m * 128, 128)
        spot = lax.broadcasted_iota(I32, (128, slots), 0) + base
        hits = one_hot(spot == slot)
        place[pl.ds(base, 128), :] = hits
        sent = dot(table, hits, (1, 1))
        sent = sent[:tall] + sent[tall:]
        a, b = pair(sent[:levels], sent[levels : 2 * levels])
        rest = sent[2 * levels :]
        msg_out[2 * m, 0:levels, :] = a
        msg_out[2 * m + 1, 0:levels, :] = b
        msg_out[2 * m, levels : levels + MSG, :] = rest
        msg_out[2 * m + 1, levels : levels + MSG, :] = turn(rest, HALF)

    def msg_copy(n, change):
        target = 2 * chip_at(n, 1) + lax.rem(core + change, 2)
        return pltpu.make_async_remote_copy(
            src_ref=msg_out.at[target],
            dst_ref=msg_in.at[lat],
            send_sem=msg_send.at[2 * n + change],
            recv_sem=msg_recv.at[2 * n + change],
            device_id={"lat": target},
            device_id_type=MESH,
        )

    def others(n):
        return (1,) if chips[n] == (0, 0) else (0, 1)


    for n in range(len(chips)):
        route(chip_at(n, 1))
        for change in others(n):
            msg_copy(n, change).start()
    msg_in[lat] = msg_out[lat]


    loads[6].wait()
    for c in range(2):
        for p in range(TILES):
            a = cour_in[c, pl.ds(p, levels, stride=ROWS), :]
            b = cour_in[c, pl.ds(p + TILES, levels, stride=ROWS), :]
            cour_t[c, p] = jnp.concatenate([a, b], axis=1)
    c_lon_out[0], c_lon_out[1] = pack_lon([cour_t[0, p] for p in range(TILES)])
    c_lat_out[0], c_lat_out[1] = pack_lat([cour_t[1, p] for p in range(TILES)])

    def edge_copies(lon_out, lon_in, lat_out, lat_in, send, recv):
        copies = []
        for i, step in enumerate((-1, 1)):
            copies.append(
                pltpu.make_async_remote_copy(
                    src_ref=lon_out.at[i],
                    dst_ref=lon_in.at[i],
                    send_sem=send.at[i],
                    recv_sem=recv.at[i],
                    device_id={"lev": lev_at(step)},
                    device_id_type=MESH,
                )
            )
        for i, step in enumerate((-1, 1)):
            copies.append(
                pltpu.make_async_remote_copy(
                    src_ref=lat_out.at[i],
                    dst_ref=lat_in.at[i],
                    send_sem=send.at[2 + i],
                    recv_sem=recv.at[2 + i],
                    device_id={"lat": lat_at(step)},
                    device_id_type=MESH,
                )
            )
        return copies

    c_copies = edge_copies(c_lon_out, c_lon_in, c_lat_out, c_lat_in, c_send, c_recv)
    for copy in c_copies:
        copy.start()


    loads[7].wait()
    loads[8].wait()
    for g in range(mat_in.shape[0] // 2):
        wide = []
        for odd in range(2):
            high, low = split(jnp.transpose(mat_in[2 * g + odd]))
            wide += [high, high, low]
        mix[pl.ds(g * levels, levels), :] = jnp.concatenate(wide, axis=1)
    tops = jnp.concatenate([top_in[0:8, :], top_in[8:16, :]], axis=1)

    first, last = lat == 0, lat == n_lat - 1
    for copy in c_copies:
        copy.wait()
    from_east, from_west = c_lon_in[0], c_lon_in[1]
    from_north, from_south = c_lat_in[0], c_lat_in[1]
    from_north = jnp.where(last, 0.0, from_north)
    from_south = jnp.where(first, 0.0, from_south)
    rows_c = [cour_t[1, p] for p in range(TILES)]
    rows_c[0] = jnp.where(low_half(rows_c[0].shape) & first, 0.0, rows_c[0])
    rows_c = extend_lat(rows_c, from_south, from_north)
    for p in range(TILES):
        here = cour_t[0, p]
        before_x, after_x, after2_x = shift_lon(here, p, from_west, from_east, (-1, 1, 2))
        lon_w = face_weights(before_x, here, after_x, after2_x)
        lat_w = face_weights(rows_c[p + 1], rows_c[p + 2], rows_c[p + 3], rows_c[p + 4])
        weights[p, 0] = 1.0 + lon_w[2] + lat_w[2]
        for i, j in enumerate((0, 1, 3, 4)):
            weights[p, 1 + i] = lon_w[j]
            weights[p, 5 + i] = lat_w[j]


    columns = TILES * 128

    def arrive(n):
        m = chip_at(n, -1)
        a, b = msg_in[2 * m], msg_in[2 * m + 1]
        one, two = pair(a[:levels], b[:levels])
        rest, _unused = pair(a[levels:], b[levels:])
        kern_rows[n, 0:levels, :] = one
        kern_rows[n, levels : 2 * levels, :] = two
        wk = jnp.concatenate([one * rest[0:1], two * rest[1:2]], axis=0)
        at = pl.ds(n * 128, 128)
        high, low = split(wk)
        weighted[0 : 2 * levels, at] = high
        weighted[2 * levels :, at] = low
        target = rest[2:3].astype(I32) - 1
        hot[:, at] = one_hot(lax.broadcasted_iota(I32, (columns, 128), 0) == target)

    group = max(1, len(chips) // 4)
    for g in range(len(chips) // group):
        for n in range(g * group, (g + 1) * group):
            for change in others(n):
                msg_copy(n, change).wait()
            arrive(n)
        taken = pl.ds(g * group * 128, group * 128)
        for q in range(TILES // 2):
            got = dot(weighted[:, taken], hot[pl.ds(q * 256, 256), taken], (1, 1))
            got = got[: 2 * levels] + got[2 * levels :]
            for t in range(2):
                for i in range(2):
                    part = got[t * levels : (t + 1) * levels, i * 128 : (i + 1) * 128]
                    if g > 0:
                        part = part + deposit[t, 2 * q + i]
                    deposit[t, 2 * q + i] = part

    def wait_fwd(t):
        def step(d, _):
            fwd_copy(t, d).wait()
            return _

        lax.fori_loop(1, n_lev, step, 0)

    a_copies = []
    for t in range(2):
        wait_fwd(t)
        for q in range(TILES // 2):
            x = jnp.concatenate(
                [
                    fwd_in[t, pl.ds(p, levels, stride=TILES), :] + deposit[t, p]
                    for p in (2 * q, 2 * q + 1)
                ],
                axis=1,
            )
            top = jnp.concatenate([tops[2 * q : 2 * q + 1], tops[2 * q + 1 : 2 * q + 2]], axis=1)
            stack = []
            for odd in range(2):
                high, low = split(jnp.where(top % 2 == odd, x, 0.0))
                stack += [high, low, high]
            mixed = dot(mix[...], jnp.concatenate(stack, axis=0))
            result = mixed[0:levels]
            for g in range(1, mat_in.shape[0] // 2):
                result = jnp.where(top // 2 == g, mixed[g * levels : (g + 1) * levels], result)
            high, low = split(result)
            conv_split[pl.ds(t * levels, levels), pl.ds(q * 256, 256)] = high
            conv_split[pl.ds((2 + t) * levels, levels), pl.ds(q * 256, 256)] = low
            conv[t, 2 * q] = result[:, :128]
            conv[t, 2 * q + 1] = result[:, 128:]
        tiles = [conv[t, p] for p in range(TILES)]
        a_lon_out[t, 0], a_lon_out[t, 1] = pack_lon(tiles)
        a_lat_out[t, 0], a_lat_out[t, 1] = pack_lat(tiles)
        a_copies.append(
            edge_copies(
                a_lon_out.at[t],
                a_lon_in.at[t],
                a_lat_out.at[t],
                a_lat_in.at[t],
                a_send.at[t],
                a_recv.at[t],
            )
        )
        for copy in a_copies[t]:
            copy.start()


    def back_copy(t, d):
        return pltpu.make_async_remote_copy(
            src_ref=back_out.at[t, block(lev_at(d)), :],
            dst_ref=back_in.at[t, block(lev), :],
            send_sem=back_send.at[t, d],
            recv_sem=back_recv.at[t, d],
            device_id={"lev": lev_at(d)},
            device_id_type=MESH,
        )

    for t in range(2):
        for copy in a_copies[t]:
            copy.wait()
        from_east, from_west = a_lon_in[t, 0], a_lon_in[t, 1]
        from_north, from_south = a_lat_in[t, 0], a_lat_in[t, 1]
        from_north = jnp.where(last, 0.0, from_north)
        from_south = jnp.where(first, 0.0, from_south)
        tiles = extend_lat([conv[t, p] for p in range(TILES)], from_south, from_north)
        for p in range(TILES):
            here = tiles[p + 2]
            around = shift_lon(here, p, from_west, from_east, (-2, -1, 1, 2))
            around += [tiles[p], tiles[p + 1], tiles[p + 3], tiles[p + 4]]
            total = weights[p, 0] * here
            for i in range(8):
                total = total + weights[p, 1 + i] * around[i]
            back_out[t, pl.ds(p, levels, stride=TILES), :] = total

        def start_back(i, _, t=t):
            back_copy(t, far(i)).start()
            return _

        lax.fori_loop(0, n_lev - 1, start_back, 0)
        back_in[t, block(lev), :] = back_out[t, block(lev), :]


    for m in range(n_lat // 4):
        picked = dot(conv_split[...], hot[:, pl.ds(m * 256, 256)])
        picked = picked[: 2 * levels] + picked[2 * levels :]
        for i in range(2):
            product = picked[:, i * 128 : (i + 1) * 128] * kern_rows[2 * m + i]
            sums = [
                jnp.sum(product[t * levels : (t + 1) * levels], axis=0, keepdims=True)
                for t in range(2)
            ]
            which = lax.broadcasted_iota(I32, (MSG, 128), 0)
            both = jnp.where(which == 0, sums[0], jnp.where(which == 1, sums[1], 0.0))
            ret_out[4 * m + 2 * i] = both
            ret_out[4 * m + 2 * i + 1] = turn(both, HALF)

    def ret_copy(n, change):
        other = lax.rem(core + change, 2)
        return pltpu.make_async_remote_copy(
            src_ref=ret_out.at[2 * n + other],
            dst_ref=ret_in.at[lat],
            send_sem=ret_send.at[2 * n + change],
            recv_sem=ret_recv.at[2 * n + change],
            device_id={"lat": 2 * chip_at(n, -1) + other},
            device_id_type=MESH,
        )


    for n in range(len(chips)):
        for change in others(n):
            ret_copy(n, change).start()
    ret_in[lat] = ret_out[n_lat - 2 + core]
    for n in range(len(chips)):
        for change in others(n):
            ret_copy(n, change).wait()

    for m in range(n_lat // 2):
        both, _unused = pair(ret_in[2 * m], ret_in[2 * m + 1])
        ret_split[:, pl.ds(m * 128, 128)] = jnp.concatenate(split(both), axis=0)
    own = dot(ret_split[...], place[...])
    own = own[:MSG] + own[MSG:]
    sens_ref[...] = own[0:2]


    for t in range(2):

        def wait_back(d, _, t=t):
            back_copy(t, d).wait()
            return _

        lax.fori_loop(1, n_lev, wait_back, 0)
        for m in range(n_lev // 2):
            for kk in range(2):
                a, b = pair(
                    back_in[t, pl.ds(m * 32 + kk * 8, 8), :],
                    back_in[t, pl.ds(m * 32 + 16 + kk * 8, 8), :],
                )
                out_ref[t, kk, 0:8, pl.ds(m * 128, 128)] = a
                out_ref[t, kk, 8:16, pl.ds(m * 128, 128)] = b


def per_device(
    n_lev,
    n_lat,
    adjoint_in,
    courant,
    cloud_top,
    conv_inverse,
    sounding_kernel,
    sounding_weight,
    sounding_owner,
    sounding_cell,
    sounding_count,
):
    levels = 2 * n_lev
    slots = sounding_kernel.shape[2]
    classes = conv_inverse.shape[0]
    columns = TILES * 128
    spots = n_lat * HALF
    operands = (
        adjoint_in,
        courant.reshape(2, levels * ROWS, HALF),
        cloud_top,
        conv_inverse,
        sounding_kernel.reshape(slots, 2 * levels).T,
        sounding_weight.reshape(slots, 2).T,
        sounding_owner.reshape(1, slots),
        sounding_cell.reshape(1, slots),
        sounding_count,
    )
    vm, dma = pltpu.VMEM, pltpu.SemaphoreType.DMA
    scratch = [vm(x.shape, x.dtype) for x in operands]
    scratch += [vm((2, n_lev * 16, 128), F32) for _ in range(4)]
    scratch += [vm((n_lat, levels + MSG, 128), F32) for _ in range(2)]
    scratch += [vm((n_lat, MSG, 128), F32) for _ in range(2)]
    scratch += [vm((2, levels, 128), F32) for _ in range(4)]
    scratch += [vm((2, 2, levels, 128), F32) for _ in range(4)]
    scratch += [
        vm((spots, slots), BF16),
        vm((n_lat // 2, 2 * levels, 128), F32),
        vm((4 * levels, spots), BF16),
        vm((columns, spots), BF16),
        vm((2, TILES, levels, 128), F32),
        vm((2, TILES, levels, 128), F32),
        vm((TILES, 9, levels, 128), F32),
        vm((classes // 2 * levels, 6 * levels), BF16),
        vm((2, TILES, levels, 128), F32),
        vm((4 * levels, columns), BF16),
        vm((2 * MSG, spots), BF16),
        dma((9,)),
    ]
    scratch += [dma((2, n_lev)) for _ in range(4)]
    scratch += [dma((n_lat,)) for _ in range(4)]
    scratch += [dma((4,)) for _ in range(2)]
    scratch += [dma((2, 4)) for _ in range(2)]
    in_hbm = pl.BlockSpec(memory_space=pltpu.HBM)
    in_vmem = pl.BlockSpec(memory_space=pltpu.VMEM)
    out, sens = pl.pallas_call(
        functools.partial(kernel, n_lev, n_lat),
        out_shape=(
            jax.ShapeDtypeStruct(adjoint_in.shape, F32),
            jax.ShapeDtypeStruct((2, slots), F32),
        ),
        in_specs=[in_hbm] * len(operands),
        out_specs=(in_vmem, in_vmem),
        scratch_shapes=scratch,
        compiler_params=pltpu.CompilerParams(
            collective_id=0, has_side_effects=True, vmem_limit_bytes=60 * 2**20
        ),
    )(*operands)
    return out, sens.T.reshape(1, 1, slots, 2)


def solution(mesh):
    placed = (
        P(None, "lev", "lat", None),
        P(None, None, "lat", "lev"),
        P("lat", "lev"),
        P(),
        P("lev", "lat", None, None),
        P("lev", "lat", None, None),
        P("lev", "lat", None),
        P("lev", "lat", None),
        P("lev", "lat"),
    )
    return jax.shard_map(
        functools.partial(per_device, mesh.shape["lev"], mesh.shape["lat"]),
        mesh=mesh,
        in_specs=placed,
        out_specs=(P(None, "lev", "lat", None), P("lev", "lat", None, None)),
        check_vma=False,
    )
```

```python
import functools

import jax
import jax.numpy as jnp
from jax import lax
from jax.experimental import pallas as pl
from jax.experimental.pallas import tpu as pltpu
from jax.sharding import PartitionSpec as P

MESH = pl.DeviceIdType.MESH
F32, BF16, I32 = jnp.float32, jnp.bfloat16, jnp.int32
ROWS = 16
TILES = 8
HALF = 64
USED = 48
SMALL = 8
MSG = 8


def lanes(shape):
    return lax.broadcasted_iota(I32, shape, len(shape) - 1)


def turn(x, shift):
    shift = shift % 128
    return x if shift == 0 else pltpu.roll(x, shift, x.ndim - 1)


def low_half(shape):
    return lanes(shape) < HALF


def pair(a, b):
    low = low_half(a.shape)
    return jnp.where(low, a, turn(b, HALF)), jnp.where(low, turn(a, HALF), b)


def split(x):
    high = x.astype(BF16)
    return high, (x - high.astype(F32)).astype(BF16)


def dot(a, b, contract=(1, 0)):
    return lax.dot_general(
        a, b, (((contract[0],), (contract[1],)), ((), ())), preferred_element_type=F32
    )


def one_hot(mask):
    return jnp.where(mask, 1.0, 0.0).astype(BF16)


def pack_lon(tiles):
    x = lanes(tiles[0].shape) % HALF
    to_west, to_east = tiles[0], turn(tiles[0], 66)
    for p in range(1, TILES):
        here = x // 2 == p
        to_west = jnp.where(here, turn(tiles[p], 2 * p), to_west)
        to_east = jnp.where(here, turn(tiles[p], 2 * p + 66), to_east)
    return to_west, to_east


def shift_lon(tile, p, from_west, from_east, steps):
    x = lanes(tile.shape) % HALF
    east = turn(from_east, HALF - 2 * p)
    west = turn(from_west, 126 - 2 * p)
    out = []
    for d in steps:
        if d > 0:
            out.append(turn(jnp.where(x < d, east, tile), -d))
        else:
            out.append(turn(jnp.where(x >= HALF + d, west, tile), -d))
    return out


def pack_lat(tiles):
    low = low_half(tiles[0].shape)
    to_south = jnp.where(low, tiles[0], turn(tiles[1], HALF))
    to_north = jnp.where(low, turn(tiles[6], HALF), tiles[7])
    return to_south, to_north


def extend_lat(tiles, from_south, from_north):
    low = low_half(tiles[0].shape)
    return (
        [
            jnp.where(low, from_south, turn(tiles[6], HALF)),
            turn(jnp.where(low, tiles[7], from_south), HALF),
        ]
        + list(tiles)
        + [
            turn(jnp.where(low, from_north, tiles[0]), HALF),
            jnp.where(low, turn(tiles[1], HALF), from_north),
        ]
    )


def face_weights(before, here, after, after2):
    def parts(c):
        pos, neg = jnp.maximum(c, 0.0), jnp.minimum(c, 0.0)
        return pos, neg, 0.25 * pos * (1.0 - pos), 0.25 * neg * (1.0 + neg)

    _, _, _, sn_before = parts(before)
    _, neg_here, sp_here, _ = parts(here)
    pos_after, _, _, sn_after = parts(after)
    _, _, sp_after2, _ = parts(after2)
    own = neg_here + sp_here
    nxt = pos_after + sn_after
    return sn_before, -own - sn_before, own - nxt, nxt + sp_after2, -sp_after2


def kernel(
    n_lev,
    n_lat,
    adj_hbm,
    cour_hbm,
    top_hbm,
    mat_hbm,
    kern_hbm,
    wt_hbm,
    owner_hbm,
    cell_hbm,
    count_hbm,
    back_in,
    sens_ref,
    adj_in,
    cour_in,
    top_in,
    mat_in,
    kern_in,
    wt_in,
    owner_in,
    cell_in,
    count_in,
    fwd_out,
    fwd_in,
    back_out,
    msg_out,
    msg_in,
    ret_out,
    ret_in,
    c_lon_out,
    c_lon_in,
    c_lat_out,
    c_lat_in,
    a_lon_out,
    a_lon_in,
    a_lat_out,
    a_lat_in,
    place,
    kern_rows,
    weighted,
    hot,
    deposit,
    cour_t,
    weights,
    mix,
    conv,
    conv_split,
    ret_split,
    in_sem,
    keep_sem,
    fwd_send,
    fwd_recv,
    back_send,
    back_recv,
    msg_send,
    msg_recv,
    ret_send,
    ret_recv,
    c_send,
    c_recv,
    a_send,
    a_recv,
):
    lev, lat = lax.axis_index("lev"), lax.axis_index("lat")
    levels = 2 * n_lev
    slots = owner_in.shape[1]

    def lev_at(d):
        return lax.rem(lev + d + n_lev, n_lev)

    def lat_at(d):
        return lax.rem(lat + d + n_lat, n_lat)

    n_y = max(2, n_lat // 8)
    n_x = n_lat // (2 * n_y)
    at_x, at_y, core = lat // (2 * n_y), lax.rem(lat // 2, n_y), lax.rem(lat, 2)

    def hops(step):
        return min(step[0], n_x - step[0]) + min(step[1], n_y - step[1])

    chips = sorted(((i, j) for i in range(n_x) for j in range(n_y)), key=hops, reverse=True)

    def chip_at(n, sign):
        i, j = chips[n]
        return lax.rem(at_x + sign * i + n_x, n_x) * n_y + lax.rem(at_y + sign * j + n_y, n_y)

    def far(i):
        half = (i + 1) // 2
        return n_lev // 2 + half * (1 - 2 * lax.rem(i, 2))

    loads = [
        pltpu.make_async_copy(source, target, in_sem.at[i])
        for i, (source, target) in enumerate(
            [
                (adj_hbm, adj_in),
                (owner_hbm, owner_in),
                (cell_hbm, cell_in),
                (count_hbm, count_in),
                (kern_hbm, kern_in),
                (wt_hbm, wt_in),
                (cour_hbm, cour_in),
                (top_hbm, top_in),
                (mat_hbm, mat_in),
            ]
        )
    ]
    for load in loads:
        load.start()

    barrier = pltpu.get_barrier_semaphore()

    def greet_lev(d, _):
        pl.semaphore_signal(barrier, inc=1, device_id={"lev": lev_at(d)}, device_id_type=MESH)
        return _

    def greet_lat(d, _):
        pl.semaphore_signal(barrier, inc=1, device_id={"lat": lat_at(d)}, device_id_type=MESH)
        return _

    lax.fori_loop(1, n_lev, greet_lev, 0)
    lax.fori_loop(1, n_lat, greet_lat, 0)

    loads[0].wait()
    for t in range(2):
        for m in range(n_lev // 2):
            for kk in range(2):
                cols = pl.ds(m * 128, 128)
                a, b = pair(adj_in[t, kk, 0:8, cols], adj_in[t, kk, 8:16, cols])
                fwd_out[t, pl.ds(m * 32 + kk * 8, 8), :] = a
                fwd_out[t, pl.ds(m * 32 + 16 + kk * 8, 8), :] = b
    pl.semaphore_wait(barrier, n_lev + n_lat - 2)


    def block(i):
        return pl.ds(pl.multiple_of(i * 16, 16), 16)

    def fwd_copy(t, d):
        return pltpu.make_async_remote_copy(
            src_ref=fwd_out.at[t, block(lev_at(d)), :],
            dst_ref=fwd_in.at[t, block(lev), :],
            send_sem=fwd_send.at[t, d],
            recv_sem=fwd_recv.at[t, d],
            device_id={"lev": lev_at(d)},
            device_id_type=MESH,
        )

    def start_fwd(t):
        def step(i, _):
            fwd_copy(t, far(i)).start()
            return _

        lax.fori_loop(0, n_lev - 1, step, 0)

    start_fwd(0)
    start_fwd(1)
    for t in range(2):
        fwd_in[t, block(lev), :] = fwd_out[t, block(lev), :]


    for i in range(1, 6):
        loads[i].wait()
    owner, cell = owner_in[...], cell_in[...]
    valid = lanes((1, slots)) < count_in[...]
    owned = (lax.broadcasted_iota(I32, (n_lat, slots), 0) == owner) & valid
    upper = one_hot(lax.broadcasted_iota(I32, (slots, slots), 0) < lanes((slots, slots)))
    before = dot(one_hot(owned), upper)
    rank = jnp.sum(jnp.where(owned, before, 0.0), axis=0, keepdims=True).astype(I32)
    slot = jnp.where(valid, owner * HALF + rank, -1)
    row = cell // HALF
    packed = (row % TILES) * 128 + (row // TILES) * HALF + cell % HALF
    which = lax.broadcasted_iota(I32, (2 * SMALL, slots), 0)
    small = jnp.where((which >= 3) & (which < 6), (packed + 1).astype(F32), 0.0)
    small = jnp.where(which < 3, wt_in[0:1, :], small)
    small = jnp.where((which >= SMALL) & (which < SMALL + 3), wt_in[1:2, :], small)
    table = jnp.concatenate([kern_in[...], small], axis=0)
    tall = 2 * levels + 2 * SMALL
    table = jnp.concatenate(split(table), axis=0)

    def route(chips_m):
        hits = []
        for m in chips_m:
            base = pl.multiple_of(m * 128, 128)
            spot = lax.broadcasted_iota(I32, (128, slots), 0) + base
            hits.append(one_hot(spot == slot))
            place[pl.ds(base, 128), :] = hits[-1]
        sent = dot(table, jnp.concatenate(hits, axis=0), (1, 1))
        sent = sent[:tall] + sent[tall:]
        for i, m in enumerate(chips_m):
            part = sent[:, i * 128 : (i + 1) * 128]
            t0 = jnp.concatenate([part[:levels], part[2 * levels : 2 * levels + SMALL]], axis=0)
            t1 = jnp.concatenate(
                [part[levels : 2 * levels], part[2 * levels + SMALL :]], axis=0
            )
            for change, full in enumerate(pair(t0, t1)):
                rest = full[levels:]
                third = lax.broadcasted_iota(I32, rest.shape, 0) % 3
                moved = jnp.where(third == 1, turn(rest, 32), turn(rest, 16))
                moved = jnp.where(third == 0, turn(rest, 48), moved)
                free = lanes(rest.shape) % HALF >= USED
                msg_out[2 * m + change, 0:SMALL, :] = jnp.where(free, moved, full[:SMALL])
                if levels > SMALL:
                    msg_out[2 * m + change, SMALL:levels, :] = full[SMALL:levels]

    def msg_copy(n, change):
        target = 2 * chip_at(n, 1) + lax.rem(core + change, 2)
        return pltpu.make_async_remote_copy(
            src_ref=msg_out.at[target],
            dst_ref=msg_in.at[lat],
            send_sem=msg_send.at[2 * n + change],
            recv_sem=msg_recv.at[2 * n + change],
            device_id={"lat": target},
            device_id_type=MESH,
        )

    def others(n):
        return (1,) if chips[n] == (0, 0) else (0, 1)


    group = max(1, len(chips) // 4)
    for g in range(0, len(chips), group):
        route([chip_at(n, 1) for n in range(g, g + group)])
        for n in range(g, g + group):
            for change in others(n):
                msg_copy(n, change).start()
    msg_in[lat] = msg_out[lat]


    loads[6].wait()
    for c in range(2):
        for p in range(TILES):
            a = cour_in[c, pl.ds(p, levels, stride=ROWS), :]
            b = cour_in[c, pl.ds(p + TILES, levels, stride=ROWS), :]
            cour_t[c, p] = jnp.concatenate([a, b], axis=1)
    c_lon_out[0], c_lon_out[1] = pack_lon([cour_t[0, p] for p in range(TILES)])
    c_lat_out[0], c_lat_out[1] = pack_lat([cour_t[1, p] for p in range(TILES)])

    def edge_copies(lon_out, lon_in, lat_out, lat_in, send, recv):
        copies = []
        for i, step in enumerate((-1, 1)):
            copies.append(
                pltpu.make_async_remote_copy(
                    src_ref=lon_out.at[i],
                    dst_ref=lon_in.at[i],
                    send_sem=send.at[i],
                    recv_sem=recv.at[i],
                    device_id={"lev": lev_at(step)},
                    device_id_type=MESH,
                )
            )
        for i, step in enumerate((-1, 1)):
            copies.append(
                pltpu.make_async_remote_copy(
                    src_ref=lat_out.at[i],
                    dst_ref=lat_in.at[i],
                    send_sem=send.at[2 + i],
                    recv_sem=recv.at[2 + i],
                    device_id={"lat": lat_at(step)},
                    device_id_type=MESH,
                )
            )
        return copies

    c_copies = edge_copies(c_lon_out, c_lon_in, c_lat_out, c_lat_in, c_send, c_recv)
    for copy in c_copies:
        copy.start()


    loads[7].wait()
    loads[8].wait()
    for g in range(mat_in.shape[0] // 2):
        wide = []
        for odd in range(2):
            high, low = split(jnp.transpose(mat_in[2 * g + odd]))
            wide += [high, high, low]
        mix[pl.ds(g * levels, levels), :] = jnp.concatenate(wide, axis=1)
    tops = jnp.concatenate([top_in[0:8, :], top_in[8:16, :]], axis=1)


    columns = TILES * 128

    def arrive(n):
        m = chip_at(n, -1)
        one, two = pair(msg_in[2 * m], msg_in[2 * m + 1])
        kern_rows[n, 0:levels, :] = one
        kern_rows[n, levels : 2 * levels, :] = two

        def small_row(rows, first):
            third = lanes((1, 128)) % HALF // 16
            out = jnp.zeros((1, 128), F32)
            for i in range(3):
                moved = turn(rows[:SMALL], 16 * i - USED)
                out = jnp.where(third == i, moved[first + i : first + i + 1], out)
            return out

        wk = jnp.concatenate([one * small_row(one, 0), two * small_row(two, 0)], axis=0)
        at = pl.ds(n * 128, 128)
        high, low = split(wk)
        weighted[0 : 2 * levels, at] = high
        weighted[2 * levels :, at] = low
        target = small_row(one, 3).astype(I32) - 1
        hot[:, at] = one_hot(lax.broadcasted_iota(I32, (columns, 128), 0) == target)

    for g in range(len(chips) // group):
        for n in range(g * group, (g + 1) * group):
            for change in others(n):
                msg_copy(n, change).wait()
            arrive(n)
        taken = pl.ds(g * group * 128, group * 128)
        for q in range(TILES // 2):
            got = dot(weighted[:, taken], hot[pl.ds(q * 256, 256), taken], (1, 1))
            got = got[: 2 * levels] + got[2 * levels :]
            for t in range(2):
                for i in range(2):
                    part = got[t * levels : (t + 1) * levels, i * 128 : (i + 1) * 128]
                    if g > 0:
                        part = part + deposit[t, 2 * q + i]
                    deposit[t, 2 * q + i] = part


    def wait_fwd(t):
        def step(d, _):
            fwd_copy(t, d).wait()
            return _

        lax.fori_loop(1, n_lev, step, 0)

    a_copies = []
    for t in range(2):
        wait_fwd(t)
        for q in range(TILES // 2):
            x = jnp.concatenate(
                [
                    fwd_in[t, pl.ds(p, levels, stride=TILES), :] + deposit[t, p]
                    for p in (2 * q, 2 * q + 1)
                ],
                axis=1,
            )
            top = jnp.concatenate([tops[2 * q : 2 * q + 1], tops[2 * q + 1 : 2 * q + 2]], axis=1)
            stack = []
            for odd in range(2):
                high, low = split(jnp.where(top % 2 == odd, x, 0.0))
                stack += [high, low, high]
            mixed = dot(mix[...], jnp.concatenate(stack, axis=0))
            result = mixed[0:levels]
            for g in range(1, mat_in.shape[0] // 2):
                result = jnp.where(top // 2 == g, mixed[g * levels : (g + 1) * levels], result)
            high, low = split(result)
            conv_split[pl.ds(t * levels, levels), pl.ds(q * 256, 256)] = high
            conv_split[pl.ds((2 + t) * levels, levels), pl.ds(q * 256, 256)] = low
            conv[t, 2 * q] = result[:, :128]
            conv[t, 2 * q + 1] = result[:, 128:]
        tiles = [conv[t, p] for p in range(TILES)]
        a_lon_out[t, 0], a_lon_out[t, 1] = pack_lon(tiles)
        a_lat_out[t, 0], a_lat_out[t, 1] = pack_lat(tiles)
        a_copies.append(
            edge_copies(
                a_lon_out.at[t],
                a_lon_in.at[t],
                a_lat_out.at[t],
                a_lat_in.at[t],
                a_send.at[t],
                a_recv.at[t],
            )
        )
        for copy in a_copies[t]:
            copy.start()

    first, last = lat == 0, lat == n_lat - 1
    for copy in c_copies:
        copy.wait()
    from_east, from_west = c_lon_in[0], c_lon_in[1]
    from_north, from_south = c_lat_in[0], c_lat_in[1]
    from_north = jnp.where(last, 0.0, from_north)
    from_south = jnp.where(first, 0.0, from_south)
    rows_c = [cour_t[1, p] for p in range(TILES)]
    rows_c[0] = jnp.where(low_half(rows_c[0].shape) & first, 0.0, rows_c[0])
    rows_c = extend_lat(rows_c, from_south, from_north)
    for p in range(TILES):
        here = cour_t[0, p]
        before_x, after_x, after2_x = shift_lon(here, p, from_west, from_east, (-1, 1, 2))
        lon_w = face_weights(before_x, here, after_x, after2_x)
        lat_w = face_weights(rows_c[p + 1], rows_c[p + 2], rows_c[p + 3], rows_c[p + 4])
        weights[p, 0] = 1.0 + lon_w[2] + lat_w[2]
        for i, j in enumerate((0, 1, 3, 4)):
            weights[p, 1 + i] = lon_w[j]
            weights[p, 5 + i] = lat_w[j]


    def back_copy(t, d):
        return pltpu.make_async_remote_copy(
            src_ref=back_out.at[t, block(lev_at(d)), :],
            dst_ref=back_in.at[t, block(lev), :],
            send_sem=back_send.at[t, d],
            recv_sem=back_recv.at[t, d],
            device_id={"lev": lev_at(d)},
            device_id_type=MESH,
        )

    keeps = []
    for t in range(2):
        for copy in a_copies[t]:
            copy.wait()
        from_east, from_west = a_lon_in[t, 0], a_lon_in[t, 1]
        from_north, from_south = a_lat_in[t, 0], a_lat_in[t, 1]
        from_north = jnp.where(last, 0.0, from_north)
        from_south = jnp.where(first, 0.0, from_south)
        tiles = extend_lat([conv[t, p] for p in range(TILES)], from_south, from_north)
        for p in range(TILES):
            here = tiles[p + 2]
            around = shift_lon(here, p, from_west, from_east, (-2, -1, 1, 2))
            around += [tiles[p], tiles[p + 1], tiles[p + 3], tiles[p + 4]]
            total = weights[p, 0] * here
            for i in range(8):
                total = total + weights[p, 1 + i] * around[i]
            back_out[t, pl.ds(p, levels, stride=TILES), :] = total

        def start_back(i, _, t=t):
            back_copy(t, far(i)).start()
            return _

        lax.fori_loop(0, n_lev - 1, start_back, 0)
        keeps.append(
            pltpu.make_async_copy(
                back_out.at[t, block(lev), :], back_in.at[t, block(lev), :], keep_sem.at[t]
            )
        )
        keeps[t].start()


    for m in range(n_lat // 4):
        picked = dot(conv_split[...], hot[:, pl.ds(m * 256, 256)])
        picked = picked[: 2 * levels] + picked[2 * levels :]
        for i in range(2):
            product = picked[:, i * 128 : (i + 1) * 128] * kern_rows[2 * m + i]
            sums = [
                jnp.sum(product[t * levels : (t + 1) * levels], axis=0, keepdims=True)
                for t in range(2)
            ]
            which = lax.broadcasted_iota(I32, (MSG, 128), 0)
            both = jnp.where(which == 0, sums[0], jnp.where(which == 1, sums[1], 0.0))
            ret_out[4 * m + 2 * i] = both
            ret_out[4 * m + 2 * i + 1] = turn(both, HALF)

    def ret_copy(n, change):
        other = lax.rem(core + change, 2)
        return pltpu.make_async_remote_copy(
            src_ref=ret_out.at[2 * n + other],
            dst_ref=ret_in.at[lat],
            send_sem=ret_send.at[2 * n + change],
            recv_sem=ret_recv.at[2 * n + change],
            device_id={"lat": 2 * chip_at(n, -1) + other},
            device_id_type=MESH,
        )


    for n in range(len(chips)):
        for change in others(n):
            ret_copy(n, change).start()
    ret_in[lat] = ret_out[n_lat - 2 + core]
    for n in range(len(chips)):
        for change in others(n):
            ret_copy(n, change).wait()

    for m in range(n_lat // 2):
        both, _unused = pair(ret_in[2 * m], ret_in[2 * m + 1])
        ret_split[:, pl.ds(m * 128, 128)] = jnp.concatenate(split(both), axis=0)
    own = dot(ret_split[...], place[...])
    own = own[:MSG] + own[MSG:]
    sens_ref[...] = own[0:2]


    for t in range(2):

        def wait_back(d, _, t=t):
            back_copy(t, d).wait()
            return _

        lax.fori_loop(1, n_lev, wait_back, 0)
        keeps[t].wait()


def finish(n_lev, back_hbm, sens_hbm, out_hbm, sens_out, back, out, load_sem, store_sem):
    loads, stores = [], []
    for t in range(2):
        loads.append(pltpu.make_async_copy(back_hbm.at[t], back.at[t], load_sem.at[t]))
        loads[t].start()
        stores.append(pltpu.make_async_copy(out.at[t], out_hbm.at[t], store_sem.at[t]))
    sens_copy = pltpu.make_async_copy(sens_hbm, sens_out, store_sem.at[2])
    sens_copy.start()
    for t in range(2):
        loads[t].wait()
        for m in range(n_lev // 2):
            for kk in range(2):
                a, b = pair(
                    back[t, pl.ds(m * 32 + kk * 8, 8), :],
                    back[t, pl.ds(m * 32 + 16 + kk * 8, 8), :],
                )
                out[t, kk, 0:8, pl.ds(m * 128, 128)] = a
                out[t, kk, 8:16, pl.ds(m * 128, 128)] = b
        stores[t].start()
    for store in stores:
        store.wait()
    sens_copy.wait()


def per_device(
    n_lev,
    n_lat,
    adjoint_in,
    courant,
    cloud_top,
    conv_inverse,
    sounding_kernel,
    sounding_weight,
    sounding_owner,
    sounding_cell,
    sounding_count,
):
    levels = 2 * n_lev
    slots = sounding_kernel.shape[2]
    classes = conv_inverse.shape[0]
    columns = TILES * 128
    spots = n_lat * HALF
    operands = (
        adjoint_in,
        courant.reshape(2, levels * ROWS, HALF),
        cloud_top,
        conv_inverse,
        sounding_kernel.reshape(slots, 2 * levels).T,
        sounding_weight.reshape(slots, 2).T,
        sounding_owner.reshape(1, slots),
        sounding_cell.reshape(1, slots),
        sounding_count,
    )
    vm, dma = pltpu.VMEM, pltpu.SemaphoreType.DMA
    scratch = [vm(x.shape, x.dtype) for x in operands]
    scratch += [vm((2, n_lev * 16, 128), F32) for _ in range(3)]
    scratch += [vm((n_lat, levels, 128), F32) for _ in range(2)]
    scratch += [vm((n_lat, MSG, 128), F32) for _ in range(2)]
    scratch += [vm((2, levels, 128), F32) for _ in range(4)]
    scratch += [vm((2, 2, levels, 128), F32) for _ in range(4)]
    scratch += [
        vm((spots, slots), BF16),
        vm((n_lat // 2, 2 * levels, 128), F32),
        vm((4 * levels, spots), BF16),
        vm((columns, spots), BF16),
        vm((2, TILES, levels, 128), F32),
        vm((2, TILES, levels, 128), F32),
        vm((TILES, 9, levels, 128), F32),
        vm((classes // 2 * levels, 6 * levels), BF16),
        vm((2, TILES, levels, 128), F32),
        vm((4 * levels, columns), BF16),
        vm((2 * MSG, spots), BF16),
        dma((9,)),
        dma((2,)),
    ]
    scratch += [dma((2, n_lev)) for _ in range(4)]
    scratch += [dma((n_lat,)) for _ in range(4)]
    scratch += [dma((4,)) for _ in range(2)]
    scratch += [dma((2, 4)) for _ in range(2)]
    in_hbm = pl.BlockSpec(memory_space=pltpu.HBM)
    in_vmem = pl.BlockSpec(memory_space=pltpu.VMEM)
    back, sens = pl.pallas_call(
        functools.partial(kernel, n_lev, n_lat),
        out_shape=(
            jax.ShapeDtypeStruct((2, n_lev * 16, 128), F32),
            jax.ShapeDtypeStruct((2, slots), F32),
        ),
        in_specs=[in_hbm] * len(operands),
        out_specs=(in_hbm, in_vmem),
        scratch_shapes=scratch,
        compiler_params=pltpu.CompilerParams(
            collective_id=0, has_side_effects=True, vmem_limit_bytes=60 * 2**20
        ),
    )(*operands)
    out, sens = pl.pallas_call(
        functools.partial(finish, n_lev),
        out_shape=(
            jax.ShapeDtypeStruct(adjoint_in.shape, F32),
            jax.ShapeDtypeStruct((2, slots), F32),
        ),
        in_specs=[in_hbm] * 2,
        out_specs=(in_hbm, in_hbm),
        scratch_shapes=[
            vm((2, n_lev * 16, 128), F32),
            vm(adjoint_in.shape, F32),
            dma((2,)),
            dma((3,)),
        ],
        compiler_params=pltpu.CompilerParams(vmem_limit_bytes=60 * 2**20),
    )(back, sens)
    return out, sens.T.reshape(1, 1, slots, 2)


def solution(mesh):
    placed = (
        P(None, "lev", "lat", None),
        P(None, None, "lat", "lev"),
        P("lat", "lev"),
        P(),
        P("lev", "lat", None, None),
        P("lev", "lat", None, None),
        P("lev", "lat", None),
        P("lev", "lat", None),
        P("lev", "lat"),
    )
    return jax.shard_map(
        functools.partial(per_device, mesh.shape["lev"], mesh.shape["lat"]),
        mesh=mesh,
        in_specs=placed,
        out_specs=(P(None, "lev", "lat", None), P("lev", "lat", None, None)),
        check_vma=False,
    )
```

```python
import functools

import jax
import jax.numpy as jnp
from jax import lax
from jax.experimental import pallas as pl
from jax.experimental.pallas import tpu as pltpu
from jax.sharding import PartitionSpec as P

MESH = pl.DeviceIdType.MESH
F32, BF16, I32 = jnp.float32, jnp.bfloat16, jnp.int32
ROWS = 16
TILES = 8
HALF = 64
USED = 48
SMALL = 8
MSG = 8


def lanes(shape):
    return lax.broadcasted_iota(I32, shape, len(shape) - 1)


def turn(x, shift):
    shift = shift % 128
    return x if shift == 0 else pltpu.roll(x, shift, x.ndim - 1)


def low_half(shape):
    return lanes(shape) < HALF


def pair(a, b):
    low = low_half(a.shape)
    return jnp.where(low, a, turn(b, HALF)), jnp.where(low, turn(a, HALF), b)


def split(x):
    high = x.astype(BF16)
    return high, (x - high.astype(F32)).astype(BF16)


def dot(a, b, contract=(1, 0)):
    return lax.dot_general(
        a, b, (((contract[0],), (contract[1],)), ((), ())), preferred_element_type=F32
    )


def one_hot(mask):
    return jnp.where(mask, 1.0, 0.0).astype(BF16)


def pack_lon(tiles):
    x = lanes(tiles[0].shape) % HALF
    to_west, to_east = tiles[0], turn(tiles[0], 66)
    for p in range(1, TILES):
        here = x // 2 == p
        to_west = jnp.where(here, turn(tiles[p], 2 * p), to_west)
        to_east = jnp.where(here, turn(tiles[p], 2 * p + 66), to_east)
    return to_west, to_east


def shift_lon(tile, p, from_west, from_east, steps):
    x = lanes(tile.shape) % HALF
    east = turn(from_east, HALF - 2 * p)
    west = turn(from_west, 126 - 2 * p)
    out = []
    for d in steps:
        if d > 0:
            out.append(turn(jnp.where(x < d, east, tile), -d))
        else:
            out.append(turn(jnp.where(x >= HALF + d, west, tile), -d))
    return out


def pack_lat(tiles):
    low = low_half(tiles[0].shape)
    to_south = jnp.where(low, tiles[0], turn(tiles[1], HALF))
    to_north = jnp.where(low, turn(tiles[6], HALF), tiles[7])
    return to_south, to_north


def extend_lat(tiles, from_south, from_north):
    low = low_half(tiles[0].shape)
    return (
        [
            jnp.where(low, from_south, turn(tiles[6], HALF)),
            turn(jnp.where(low, tiles[7], from_south), HALF),
        ]
        + list(tiles)
        + [
            turn(jnp.where(low, from_north, tiles[0]), HALF),
            jnp.where(low, turn(tiles[1], HALF), from_north),
        ]
    )


def face_weights(before, here, after, after2):
    def parts(c):
        pos, neg = jnp.maximum(c, 0.0), jnp.minimum(c, 0.0)
        return pos, neg, 0.25 * pos * (1.0 - pos), 0.25 * neg * (1.0 + neg)

    _, _, _, sn_before = parts(before)
    _, neg_here, sp_here, _ = parts(here)
    pos_after, _, _, sn_after = parts(after)
    _, _, sp_after2, _ = parts(after2)
    own = neg_here + sp_here
    nxt = pos_after + sn_after
    return sn_before, -own - sn_before, own - nxt, nxt + sp_after2, -sp_after2


def kernel(
    n_lev,
    n_lat,
    adj_hbm,
    cour_hbm,
    top_hbm,
    mat_hbm,
    kern_hbm,
    wt_hbm,
    owner_hbm,
    cell_hbm,
    count_ref,
    back_in,
    sens_ref,
    adj_in,
    cour_in,
    top_in,
    mat_in,
    kern_in,
    wt_in,
    owner_in,
    cell_in,
    fwd_out,
    fwd_in,
    back_out,
    msg_out,
    msg_in,
    ret_out,
    ret_in,
    c_lon_out,
    c_lon_in,
    c_lat_out,
    c_lat_in,
    a_lon_out,
    a_lon_in,
    a_lat_out,
    a_lat_in,
    place,
    kern_rows,
    weighted,
    hot,
    deposit,
    cour_t,
    weights,
    mix,
    conv,
    conv_split,
    ret_split,
    in_sem,
    keep_sem,
    fwd_send,
    fwd_recv,
    back_send,
    back_recv,
    msg_send,
    msg_recv,
    ret_send,
    ret_recv,
    c_send,
    c_recv,
    a_send,
    a_recv,
):
    lev, lat = lax.axis_index("lev"), lax.axis_index("lat")
    levels = 2 * n_lev
    slots = owner_in.shape[1]

    def lev_at(d):
        return lax.rem(lev + d + n_lev, n_lev)

    def lat_at(d):
        return lax.rem(lat + d + n_lat, n_lat)

    n_y = max(2, n_lat // 8)
    n_x = n_lat // (2 * n_y)
    at_x, at_y, core = lat // (2 * n_y), lax.rem(lat // 2, n_y), lax.rem(lat, 2)

    def hops(step):
        return min(step[0], n_x - step[0]) + min(step[1], n_y - step[1])

    chips = sorted(((i, j) for i in range(n_x) for j in range(n_y)), key=hops)

    def chip_at(n, sign):
        i, j = chips[n]
        return lax.rem(at_x + sign * i + n_x, n_x) * n_y + lax.rem(at_y + sign * j + n_y, n_y)

    def far(i):
        half = (i + 1) // 2
        return n_lev // 2 + half * (1 - 2 * lax.rem(i, 2))

    loads = [
        pltpu.make_async_copy(source, target, in_sem.at[i])
        for i, (source, target) in enumerate(
            [
                (adj_hbm, adj_in),
                (owner_hbm, owner_in),
                (cell_hbm, cell_in),
                (kern_hbm, kern_in),
                (wt_hbm, wt_in),
                (cour_hbm, cour_in),
                (top_hbm, top_in),
                (mat_hbm, mat_in),
            ]
        )
    ]
    for load in loads:
        load.start()

    barrier = pltpu.get_barrier_semaphore()

    def greet_lev(d, _):
        pl.semaphore_signal(barrier, inc=1, device_id={"lev": lev_at(far(d))}, device_id_type=MESH)
        return _

    def greet_lat(d, _):
        pl.semaphore_signal(barrier, inc=1, device_id={"lat": lat_at(d)}, device_id_type=MESH)
        return _

    lax.fori_loop(0, n_lev - 1, greet_lev, 0)
    lax.fori_loop(1, n_lat, greet_lat, 0)

    loads[0].wait()
    for t in range(2):
        for m in range(n_lev // 2):
            for kk in range(2):
                cols = pl.ds(m * 128, 128)
                a, b = pair(adj_in[t, kk, 0:8, cols], adj_in[t, kk, 8:16, cols])
                fwd_out[t, pl.ds(m * 32 + kk * 8, 8), :] = a
                fwd_out[t, pl.ds(m * 32 + 16 + kk * 8, 8), :] = b
    for i in range(1, 5):
        loads[i].wait()
    owner, cell = owner_in[...], cell_in[...]
    valid = lanes((1, slots)) < count_ref[0, 0]
    owned = (lax.broadcasted_iota(I32, (n_lat, slots), 0) == owner) & valid
    upper = one_hot(lax.broadcasted_iota(I32, (slots, slots), 0) < lanes((slots, slots)))
    before = dot(one_hot(owned), upper)
    rank = jnp.sum(jnp.where(owned, before, 0.0), axis=0, keepdims=True).astype(I32)
    slot = jnp.where(valid, owner * HALF + rank, -1)
    row = cell // HALF
    packed = (row % TILES) * 128 + (row // TILES) * HALF + cell % HALF
    which = lax.broadcasted_iota(I32, (2 * SMALL, slots), 0)
    small = jnp.where((which >= 3) & (which < 6), (packed + 1).astype(F32), 0.0)
    small = jnp.where(which < 3, wt_in[0:1, :], small)
    small = jnp.where((which >= SMALL) & (which < SMALL + 3), wt_in[1:2, :], small)
    table = jnp.concatenate([kern_in[...], small], axis=0)
    tall = 2 * levels + 2 * SMALL
    table = jnp.concatenate(split(table), axis=0)

    def route(chips_m):
        hits = []
        for m in chips_m:
            base = pl.multiple_of(m * 128, 128)
            spot = lax.broadcasted_iota(I32, (128, slots), 0) + base
            hits.append(one_hot(spot == slot))
            place[pl.ds(base, 128), :] = hits[-1]
        sent = dot(table, jnp.concatenate(hits, axis=0), (1, 1))
        sent = sent[:tall] + sent[tall:]
        for i, m in enumerate(chips_m):
            part = sent[:, i * 128 : (i + 1) * 128]
            t0 = jnp.concatenate([part[:levels], part[2 * levels : 2 * levels + SMALL]], axis=0)
            t1 = jnp.concatenate(
                [part[levels : 2 * levels], part[2 * levels + SMALL :]], axis=0
            )
            for change, full in enumerate(pair(t0, t1)):
                rest = full[levels:]
                third = lax.broadcasted_iota(I32, rest.shape, 0) % 3
                moved = jnp.where(third == 1, turn(rest, 32), turn(rest, 16))
                moved = jnp.where(third == 0, turn(rest, 48), moved)
                free = lanes(rest.shape) % HALF >= USED
                msg_out[2 * m + change, 0:SMALL, :] = jnp.where(free, moved, full[:SMALL])
                if levels > SMALL:
                    msg_out[2 * m + change, SMALL:levels, :] = full[SMALL:levels]

    group = max(1, len(chips) // 4)
    for g in range(0, len(chips), group):
        route([chip_at(n, 1) for n in range(g, g + group)])

    loads[5].wait()
    for c in range(2):
        for p in range(TILES):
            a = cour_in[c, pl.ds(p, levels, stride=ROWS), :]
            b = cour_in[c, pl.ds(p + TILES, levels, stride=ROWS), :]
            cour_t[c, p] = jnp.concatenate([a, b], axis=1)
    c_lon_out[0], c_lon_out[1] = pack_lon([cour_t[0, p] for p in range(TILES)])
    c_lat_out[0], c_lat_out[1] = pack_lat([cour_t[1, p] for p in range(TILES)])

    def edge_copies(lon_out, lon_in, lat_out, lat_in, send, recv):
        copies = []
        for i, step in enumerate((-1, 1)):
            copies.append(
                pltpu.make_async_remote_copy(
                    src_ref=lon_out.at[i],
                    dst_ref=lon_in.at[i],
                    send_sem=send.at[i],
                    recv_sem=recv.at[i],
                    device_id={"lev": lev_at(step)},
                    device_id_type=MESH,
                )
            )
        for i, step in enumerate((-1, 1)):
            copies.append(
                pltpu.make_async_remote_copy(
                    src_ref=lat_out.at[i],
                    dst_ref=lat_in.at[i],
                    send_sem=send.at[2 + i],
                    recv_sem=recv.at[2 + i],
                    device_id={"lat": lat_at(step)},
                    device_id_type=MESH,
                )
            )
        return copies

    c_copies = edge_copies(c_lon_out, c_lon_in, c_lat_out, c_lat_in, c_send, c_recv)

    def block(i):
        return pl.ds(pl.multiple_of(i * 16, 16), 16)

    def fwd_copy(t, d):
        return pltpu.make_async_remote_copy(
            src_ref=fwd_out.at[t, block(lev_at(d)), :],
            dst_ref=fwd_in.at[t, block(lev), :],
            send_sem=fwd_send.at[t, d],
            recv_sem=fwd_recv.at[t, d],
            device_id={"lev": lev_at(d)},
            device_id_type=MESH,
        )

    def start_fwd(t):
        def step(i, _):
            fwd_copy(t, far(i)).start()
            return _

        lax.fori_loop(0, n_lev - 1, step, 0)

    def msg_copy(n, change):
        target = 2 * chip_at(n, 1) + lax.rem(core + change, 2)
        return pltpu.make_async_remote_copy(
            src_ref=msg_out.at[target],
            dst_ref=msg_in.at[lat],
            send_sem=msg_send.at[2 * n + change],
            recv_sem=msg_recv.at[2 * n + change],
            device_id={"lat": target},
            device_id_type=MESH,
        )

    def others(n):
        return (1,) if chips[n] == (0, 0) else (0, 1)


    pl.semaphore_wait(barrier, n_lev + n_lat - 2)

    start_fwd(0)
    for n in range(len(chips)):
        for change in others(n):
            msg_copy(n, change).start()
    start_fwd(1)
    for copy in c_copies:
        copy.start()
    for t in range(2):
        fwd_in[t, block(lev), :] = fwd_out[t, block(lev), :]
    msg_in[lat] = msg_out[lat]


    loads[6].wait()
    loads[7].wait()
    for g in range(mat_in.shape[0] // 2):
        wide = []
        for odd in range(2):
            high, low = split(jnp.transpose(mat_in[2 * g + odd]))
            wide += [high, high, low]
        mix[pl.ds(g * levels, levels), :] = jnp.concatenate(wide, axis=1)
    tops = jnp.concatenate([top_in[0:8, :], top_in[8:16, :]], axis=1)


    columns = TILES * 128

    def arrive(n):
        m = chip_at(n, -1)
        one, two = pair(msg_in[2 * m], msg_in[2 * m + 1])
        kern_rows[n, 0:levels, :] = one
        kern_rows[n, levels : 2 * levels, :] = two

        def small_row(rows, first):
            third = lanes((1, 128)) % HALF // 16
            out = jnp.zeros((1, 128), F32)
            for i in range(3):
                moved = turn(rows[:SMALL], 16 * i - USED)
                out = jnp.where(third == i, moved[first + i : first + i + 1], out)
            return out

        wk = jnp.concatenate([one * small_row(one, 0), two * small_row(two, 0)], axis=0)
        at = pl.ds(n * 128, 128)
        high, low = split(wk)
        weighted[0 : 2 * levels, at] = high
        weighted[2 * levels :, at] = low
        target = small_row(one, 3).astype(I32) - 1
        hot[:, at] = one_hot(lax.broadcasted_iota(I32, (columns, 128), 0) == target)


    group = max(1, len(chips) // 2)
    for g in range(len(chips) // group):
        for n in range(g * group, (g + 1) * group):
            for change in others(n):
                msg_copy(n, change).wait()
        for n in range(g * group, (g + 1) * group):
            arrive(n)
        taken = pl.ds(g * group * 128, group * 128)
        for q in range(TILES // 2):
            got = dot(weighted[:, taken], hot[pl.ds(q * 256, 256), taken], (1, 1))
            got = got[: 2 * levels] + got[2 * levels :]
            for t in range(2):
                for i in range(2):
                    part = got[t * levels : (t + 1) * levels, i * 128 : (i + 1) * 128]
                    if g > 0:
                        part = part + deposit[t, 2 * q + i]
                    deposit[t, 2 * q + i] = part


    def wait_fwd(t):
        def step(d, _):
            fwd_copy(t, d).wait()
            return _

        lax.fori_loop(1, n_lev, step, 0)

    a_copies = []
    for t in range(2):
        wait_fwd(t)
        for q in range(TILES // 2):
            x = jnp.concatenate(
                [
                    fwd_in[t, pl.ds(p, levels, stride=TILES), :] + deposit[t, p]
                    for p in (2 * q, 2 * q + 1)
                ],
                axis=1,
            )
            top = jnp.concatenate([tops[2 * q : 2 * q + 1], tops[2 * q + 1 : 2 * q + 2]], axis=1)
            stack = []
            for odd in range(2):
                high, low = split(jnp.where(top % 2 == odd, x, 0.0))
                stack += [high, low, high]
            mixed = dot(mix[...], jnp.concatenate(stack, axis=0))
            result = mixed[0:levels]
            for g in range(1, mat_in.shape[0] // 2):
                result = jnp.where(top // 2 == g, mixed[g * levels : (g + 1) * levels], result)
            high, low = split(result)
            conv_split[pl.ds(t * levels, levels), pl.ds(q * 256, 256)] = high
            conv_split[pl.ds((2 + t) * levels, levels), pl.ds(q * 256, 256)] = low
            conv[t, 2 * q] = result[:, :128]
            conv[t, 2 * q + 1] = result[:, 128:]
        tiles = [conv[t, p] for p in range(TILES)]
        a_lon_out[t, 0], a_lon_out[t, 1] = pack_lon(tiles)
        a_lat_out[t, 0], a_lat_out[t, 1] = pack_lat(tiles)
        a_copies.append(
            edge_copies(
                a_lon_out.at[t],
                a_lon_in.at[t],
                a_lat_out.at[t],
                a_lat_in.at[t],
                a_send.at[t],
                a_recv.at[t],
            )
        )
        for copy in a_copies[t]:
            copy.start()

    first, last = lat == 0, lat == n_lat - 1
    for copy in c_copies:
        copy.wait()
    from_east, from_west = c_lon_in[0], c_lon_in[1]
    from_north, from_south = c_lat_in[0], c_lat_in[1]
    from_north = jnp.where(last, 0.0, from_north)
    from_south = jnp.where(first, 0.0, from_south)
    rows_c = [cour_t[1, p] for p in range(TILES)]
    rows_c[0] = jnp.where(low_half(rows_c[0].shape) & first, 0.0, rows_c[0])
    rows_c = extend_lat(rows_c, from_south, from_north)
    for p in range(TILES):
        here = cour_t[0, p]
        before_x, after_x, after2_x = shift_lon(here, p, from_west, from_east, (-1, 1, 2))
        lon_w = face_weights(before_x, here, after_x, after2_x)
        lat_w = face_weights(rows_c[p + 1], rows_c[p + 2], rows_c[p + 3], rows_c[p + 4])
        weights[p, 0] = 1.0 + lon_w[2] + lat_w[2]
        for i, j in enumerate((0, 1, 3, 4)):
            weights[p, 1 + i] = lon_w[j]
            weights[p, 5 + i] = lat_w[j]


    def back_copy(t, d):
        return pltpu.make_async_remote_copy(
            src_ref=back_out.at[t, block(lev_at(d)), :],
            dst_ref=back_in.at[t, block(lev), :],
            send_sem=back_send.at[t, d],
            recv_sem=back_recv.at[t, d],
            device_id={"lev": lev_at(d)},
            device_id_type=MESH,
        )

    keeps = []
    for t in range(2):
        for copy in a_copies[t]:
            copy.wait()
        from_east, from_west = a_lon_in[t, 0], a_lon_in[t, 1]
        from_north, from_south = a_lat_in[t, 0], a_lat_in[t, 1]
        from_north = jnp.where(last, 0.0, from_north)
        from_south = jnp.where(first, 0.0, from_south)
        tiles = extend_lat([conv[t, p] for p in range(TILES)], from_south, from_north)
        for p in range(TILES):
            here = tiles[p + 2]
            around = shift_lon(here, p, from_west, from_east, (-2, -1, 1, 2))
            around += [tiles[p], tiles[p + 1], tiles[p + 3], tiles[p + 4]]
            total = weights[p, 0] * here
            for i in range(8):
                total = total + weights[p, 1 + i] * around[i]
            back_out[t, pl.ds(p, levels, stride=TILES), :] = total

        def start_back(i, _, t=t):
            back_copy(t, far(i)).start()
            return _

        lax.fori_loop(0, n_lev - 1, start_back, 0)
        keeps.append(
            pltpu.make_async_copy(
                back_out.at[t, block(lev), :], back_in.at[t, block(lev), :], keep_sem.at[t]
            )
        )
        keeps[t].start()


    for m in range(n_lat // 4):
        picked = dot(conv_split[...], hot[:, pl.ds(m * 256, 256)])
        picked = picked[: 2 * levels] + picked[2 * levels :]
        for i in range(2):
            product = picked[:, i * 128 : (i + 1) * 128] * kern_rows[2 * m + i]
            sums = [
                jnp.sum(product[t * levels : (t + 1) * levels], axis=0, keepdims=True)
                for t in range(2)
            ]
            which = lax.broadcasted_iota(I32, (MSG, 128), 0)
            both = jnp.where(which == 0, sums[0], jnp.where(which == 1, sums[1], 0.0))
            ret_out[4 * m + 2 * i] = both
            ret_out[4 * m + 2 * i + 1] = turn(both, HALF)

    def ret_copy(n, change):
        other = lax.rem(core + change, 2)
        return pltpu.make_async_remote_copy(
            src_ref=ret_out.at[2 * n + other],
            dst_ref=ret_in.at[lat],
            send_sem=ret_send.at[2 * n + change],
            recv_sem=ret_recv.at[2 * n + change],
            device_id={"lat": 2 * chip_at(n, -1) + other},
            device_id_type=MESH,
        )


    for n in range(len(chips)):
        for change in others(n):
            ret_copy(n, change).start()
    ret_in[lat] = ret_out[core]
    for n in range(len(chips)):
        for change in others(n):
            ret_copy(n, change).wait()

    for m in range(n_lat // 2):
        both, _unused = pair(ret_in[2 * m], ret_in[2 * m + 1])
        ret_split[:, pl.ds(m * 128, 128)] = jnp.concatenate(split(both), axis=0)
    own = dot(ret_split[...], place[...])
    own = own[:MSG] + own[MSG:]
    sens_ref[...] = own[0:2]


    for t in range(2):

        def wait_back(d, _, t=t):
            back_copy(t, d).wait()
            return _

        lax.fori_loop(1, n_lev, wait_back, 0)
        keeps[t].wait()


def finish(n_lev, back_hbm, sens_hbm, out_hbm, sens_out, back, out, load_sem, store_sem):
    loads, stores = [], []
    for t in range(2):
        loads.append(pltpu.make_async_copy(back_hbm.at[t], back.at[t], load_sem.at[t]))
        loads[t].start()
        stores.append(pltpu.make_async_copy(out.at[t], out_hbm.at[t], store_sem.at[t]))
    sens_copy = pltpu.make_async_copy(sens_hbm, sens_out, store_sem.at[2])
    sens_copy.start()
    for t in range(2):
        loads[t].wait()
        for m in range(n_lev // 2):
            for kk in range(2):
                a, b = pair(
                    back[t, pl.ds(m * 32 + kk * 8, 8), :],
                    back[t, pl.ds(m * 32 + 16 + kk * 8, 8), :],
                )
                out[t, kk, 0:8, pl.ds(m * 128, 128)] = a
                out[t, kk, 8:16, pl.ds(m * 128, 128)] = b
        stores[t].start()
    for store in stores:
        store.wait()
    sens_copy.wait()


def per_device(
    n_lev,
    n_lat,
    adjoint_in,
    courant,
    cloud_top,
    conv_inverse,
    sounding_kernel,
    sounding_weight,
    sounding_owner,
    sounding_cell,
    sounding_count,
):
    levels = 2 * n_lev
    slots = sounding_kernel.shape[2]
    classes = conv_inverse.shape[0]
    columns = TILES * 128
    spots = n_lat * HALF
    operands = (
        adjoint_in,
        courant.reshape(2, levels * ROWS, HALF),
        cloud_top,
        conv_inverse,
        sounding_kernel.reshape(slots, 2 * levels).T,
        sounding_weight.reshape(slots, 2).T,
        sounding_owner.reshape(1, slots),
        sounding_cell.reshape(1, slots),
        sounding_count,
    )
    vm, dma = pltpu.VMEM, pltpu.SemaphoreType.DMA
    scratch = [vm(x.shape, x.dtype) for x in operands[:-1]]
    scratch += [vm((2, n_lev * 16, 128), F32) for _ in range(3)]
    scratch += [vm((n_lat, levels, 128), F32) for _ in range(2)]
    scratch += [vm((n_lat, MSG, 128), F32) for _ in range(2)]
    scratch += [vm((2, levels, 128), F32) for _ in range(4)]
    scratch += [vm((2, 2, levels, 128), F32) for _ in range(4)]
    scratch += [
        vm((spots, slots), BF16),
        vm((n_lat // 2, 2 * levels, 128), F32),
        vm((4 * levels, spots), BF16),
        vm((columns, spots), BF16),
        vm((2, TILES, levels, 128), F32),
        vm((2, TILES, levels, 128), F32),
        vm((TILES, 9, levels, 128), F32),
        vm((classes // 2 * levels, 6 * levels), BF16),
        vm((2, TILES, levels, 128), F32),
        vm((4 * levels, columns), BF16),
        vm((2 * MSG, spots), BF16),
        dma((8,)),
        dma((2,)),
    ]
    scratch += [dma((2, n_lev)) for _ in range(4)]
    scratch += [dma((n_lat,)) for _ in range(4)]
    scratch += [dma((4,)) for _ in range(2)]
    scratch += [dma((2, 4)) for _ in range(2)]
    in_hbm = pl.BlockSpec(memory_space=pltpu.HBM)
    in_vmem = pl.BlockSpec(memory_space=pltpu.VMEM)
    back, sens = pl.pallas_call(
        functools.partial(kernel, n_lev, n_lat),
        out_shape=(
            jax.ShapeDtypeStruct((2, n_lev * 16, 128), F32),
            jax.ShapeDtypeStruct((2, slots), F32),
        ),
        in_specs=[in_hbm] * (len(operands) - 1) + [pl.BlockSpec(memory_space=pltpu.SMEM)],
        out_specs=(in_hbm, in_vmem),
        scratch_shapes=scratch,
        compiler_params=pltpu.CompilerParams(
            collective_id=0, has_side_effects=True, vmem_limit_bytes=60 * 2**20
        ),
    )(*operands)
    out, sens = pl.pallas_call(
        functools.partial(finish, n_lev),
        out_shape=(
            jax.ShapeDtypeStruct(adjoint_in.shape, F32),
            jax.ShapeDtypeStruct((2, slots), F32),
        ),
        in_specs=[in_hbm] * 2,
        out_specs=(in_hbm, in_hbm),
        scratch_shapes=[
            vm((2, n_lev * 16, 128), F32),
            vm(adjoint_in.shape, F32),
            dma((2,)),
            dma((3,)),
        ],
        compiler_params=pltpu.CompilerParams(vmem_limit_bytes=60 * 2**20),
    )(back, sens)
    return out, sens.T.reshape(1, 1, slots, 2)


def solution(mesh):
    placed = (
        P(None, "lev", "lat", None),
        P(None, None, "lat", "lev"),
        P("lat", "lev"),
        P(),
        P("lev", "lat", None, None),
        P("lev", "lat", None, None),
        P("lev", "lat", None),
        P("lev", "lat", None),
        P("lev", "lat"),
    )
    return jax.shard_map(
        functools.partial(per_device, mesh.shape["lev"], mesh.shape["lat"]),
        mesh=mesh,
        in_specs=placed,
        out_specs=(P(None, "lev", "lat", None), P("lev", "lat", None, None)),
        check_vma=False,
    )
```

```python
import functools

import jax
import jax.numpy as jnp
from jax import lax
from jax.experimental import pallas as pl
from jax.experimental.pallas import tpu as pltpu
from jax.sharding import PartitionSpec as P

MESH = pl.DeviceIdType.MESH
F32, BF16, I32 = jnp.float32, jnp.bfloat16, jnp.int32
ROWS = 16
TILES = 8
HALF = 64
USED = 48
SMALL = 8
MSG = 8


def lanes(shape):
    return lax.broadcasted_iota(I32, shape, len(shape) - 1)


def turn(x, shift):
    shift = shift % 128
    return x if shift == 0 else pltpu.roll(x, shift, x.ndim - 1)


def low_half(shape):
    return lanes(shape) < HALF


def pair(a, b):
    low = low_half(a.shape)
    return jnp.where(low, a, turn(b, HALF)), jnp.where(low, turn(a, HALF), b)


def split(x):
    high = x.astype(BF16)
    return high, (x - high.astype(F32)).astype(BF16)


def dot(a, b, contract=(1, 0)):
    return lax.dot_general(
        a, b, (((contract[0],), (contract[1],)), ((), ())), preferred_element_type=F32
    )


def one_hot(mask):
    return jnp.where(mask, 1.0, 0.0).astype(BF16)


def pack_lon(tiles):
    x = lanes(tiles[0].shape) % HALF
    to_west, to_east = tiles[0], turn(tiles[0], 66)
    for p in range(1, TILES):
        here = x // 2 == p
        to_west = jnp.where(here, turn(tiles[p], 2 * p), to_west)
        to_east = jnp.where(here, turn(tiles[p], 2 * p + 66), to_east)
    return tuple(fold(edge) for edge in (to_west, to_east))


def fold(edge):
    out = edge[0:8]
    for i in range(1, edge.shape[0] // 8):
        here = lanes(out.shape) % HALF // 16 == i
        out = jnp.where(here, turn(edge[8 * i : 8 * i + 8], 16 * i), out)
    return out


def unfold(edge, levels):
    return jnp.concatenate([turn(edge, -16 * i) for i in range(levels // 8)], axis=0)


def shift_lon(tile, p, from_west, from_east, steps):
    x = lanes(tile.shape) % HALF
    east = turn(from_east, HALF - 2 * p)
    west = turn(from_west, 126 - 2 * p)
    out = []
    for d in steps:
        if d > 0:
            out.append(turn(jnp.where(x < d, east, tile), -d))
        else:
            out.append(turn(jnp.where(x >= HALF + d, west, tile), -d))
    return out


def pack_lat(tiles):
    low = low_half(tiles[0].shape)
    to_south = jnp.where(low, tiles[0], turn(tiles[1], HALF))
    to_north = jnp.where(low, turn(tiles[6], HALF), tiles[7])
    return to_south, to_north


def extend_lat(tiles, from_south, from_north):
    low = low_half(tiles[0].shape)
    return (
        [
            jnp.where(low, from_south, turn(tiles[6], HALF)),
            turn(jnp.where(low, tiles[7], from_south), HALF),
        ]
        + list(tiles)
        + [
            turn(jnp.where(low, from_north, tiles[0]), HALF),
            jnp.where(low, turn(tiles[1], HALF), from_north),
        ]
    )


def face_weights(before, here, after, after2):
    def parts(c):
        pos, neg = jnp.maximum(c, 0.0), jnp.minimum(c, 0.0)
        return pos, neg, 0.25 * pos * (1.0 - pos), 0.25 * neg * (1.0 + neg)

    _, _, _, sn_before = parts(before)
    _, neg_here, sp_here, _ = parts(here)
    pos_after, _, _, sn_after = parts(after)
    _, _, sp_after2, _ = parts(after2)
    own = neg_here + sp_here
    nxt = pos_after + sn_after
    return sn_before, -own - sn_before, own - nxt, nxt + sp_after2, -sp_after2


def kernel(
    n_lev,
    n_lat,
    adj_hbm,
    cour_hbm,
    top_hbm,
    mat_hbm,
    kern_hbm,
    wt_hbm,
    owner_hbm,
    cell_hbm,
    count_ref,
    back_in,
    sens_out,
    adj_in,
    cour_in,
    top_in,
    mat_in,
    kern_in,
    wt_in,
    owner_in,
    cell_in,
    fwd_out,
    fwd_in,
    back_out,
    msg_out,
    msg_in,
    ret_out,
    ret_in,
    c_lon_out,
    c_lon_in,
    c_lat_out,
    c_lat_in,
    a_lon_out,
    a_lon_in,
    a_lat_out,
    a_lat_in,
    place,
    kern_rows,
    weighted,
    hot,
    deposit,
    cour_t,
    weights,
    mix,
    conv,
    conv_split,
    ret_split,
    sens,
    in_sem,
    keep_sem,
    fwd_send,
    fwd_recv,
    back_send,
    back_recv,
    msg_send,
    msg_recv,
    ret_send,
    ret_recv,
    c_send,
    c_recv,
    a_send,
    a_recv,
):
    lev, lat = lax.axis_index("lev"), lax.axis_index("lat")
    levels = 2 * n_lev
    slots = owner_in.shape[1]

    def lev_at(d):
        return lax.rem(lev + d + n_lev, n_lev)

    def lat_at(d):
        return lax.rem(lat + d + n_lat, n_lat)

    n_y = max(2, n_lat // 8)
    n_x = n_lat // (2 * n_y)
    at_x, at_y, core = lat // (2 * n_y), lax.rem(lat // 2, n_y), lax.rem(lat, 2)

    def hops(step):
        return min(step[0], n_x - step[0]) + min(step[1], n_y - step[1])

    chips = sorted(((i, j) for i in range(n_x) for j in range(n_y)), key=hops)

    def chip_at(n, sign):
        i, j = chips[n]
        return lax.rem(at_x + sign * i + n_x, n_x) * n_y + lax.rem(at_y + sign * j + n_y, n_y)

    def far(i):
        half = (i + 1) // 2
        return n_lev // 2 + half * (1 - 2 * (i % 2))

    loads = [
        pltpu.make_async_copy(source, target, in_sem.at[i])
        for i, (source, target) in enumerate(
            [
                (adj_hbm, adj_in),
                (owner_hbm, owner_in),
                (cell_hbm, cell_in),
                (kern_hbm, kern_in),
                (wt_hbm, wt_in),
                (cour_hbm, cour_in),
                (top_hbm, top_in),
                (mat_hbm, mat_in),
            ]
        )
    ]
    for load in loads:
        load.start()

    barrier = pltpu.get_barrier_semaphore()

    def greet_lev(d, _):
        pl.semaphore_signal(barrier, inc=1, device_id={"lev": lev_at(far(d))}, device_id_type=MESH)
        return _

    def greet_lat(d, _):
        pl.semaphore_signal(barrier, inc=1, device_id={"lat": lat_at(d)}, device_id_type=MESH)
        return _

    lax.fori_loop(0, n_lev - 1, greet_lev, 0)
    lax.fori_loop(1, n_lat, greet_lat, 0)

    loads[0].wait()
    for t in range(2):
        for m in range(n_lev // 2):
            for kk in range(2):
                cols = pl.ds(m * 128, 128)
                a, b = pair(adj_in[t, kk, 0:8, cols], adj_in[t, kk, 8:16, cols])
                fwd_out[t, pl.ds(m * 32 + kk * 8, 8), :] = a
                fwd_out[t, pl.ds(m * 32 + 16 + kk * 8, 8), :] = b
    for i in range(1, 5):
        loads[i].wait()
    owner, cell = owner_in[...], cell_in[...]
    valid = lanes((1, slots)) < count_ref[0, 0]
    owned = (lax.broadcasted_iota(I32, (n_lat, slots), 0) == owner) & valid
    upper = one_hot(lax.broadcasted_iota(I32, (slots, slots), 0) < lanes((slots, slots)))
    before = dot(one_hot(owned), upper)
    rank = jnp.sum(jnp.where(owned, before, 0.0), axis=0, keepdims=True).astype(I32)
    slot = jnp.where(valid, owner * HALF + rank, -1)
    row = cell // HALF
    packed = (row % TILES) * 128 + (row // TILES) * HALF + cell % HALF
    which = lax.broadcasted_iota(I32, (2 * SMALL, slots), 0)
    small = jnp.where((which >= 3) & (which < 6), (packed + 1).astype(F32), 0.0)
    small = jnp.where(which < 3, wt_in[0:1, :], small)
    small = jnp.where((which >= SMALL) & (which < SMALL + 3), wt_in[1:2, :], small)
    table = jnp.concatenate([kern_in[...], small], axis=0)
    tall = 2 * levels + 2 * SMALL
    table = jnp.concatenate(split(table), axis=0)

    def route(chips_m):
        hits = []
        for m in chips_m:
            base = pl.multiple_of(m * 128, 128)
            spot = lax.broadcasted_iota(I32, (128, slots), 0) + base
            hits.append(one_hot(spot == slot))
            place[pl.ds(base, 128), :] = hits[-1]
        sent = dot(table, jnp.concatenate(hits, axis=0), (1, 1))
        sent = sent[:tall] + sent[tall:]
        for i, m in enumerate(chips_m):
            part = sent[:, i * 128 : (i + 1) * 128]
            t0 = jnp.concatenate([part[:levels], part[2 * levels : 2 * levels + SMALL]], axis=0)
            t1 = jnp.concatenate(
                [part[levels : 2 * levels], part[2 * levels + SMALL :]], axis=0
            )
            for change, full in enumerate(pair(t0, t1)):
                rest = full[levels:]
                third = lax.broadcasted_iota(I32, rest.shape, 0) % 3
                moved = jnp.where(third == 1, turn(rest, 32), turn(rest, 16))
                moved = jnp.where(third == 0, turn(rest, 48), moved)
                free = lanes(rest.shape) % HALF >= USED
                msg_out[2 * m + change, 0:SMALL, :] = jnp.where(free, moved, full[:SMALL])
                if levels > SMALL:
                    msg_out[2 * m + change, SMALL:levels, :] = full[SMALL:levels]

    group = max(1, len(chips) // 4)
    for g in range(0, len(chips), group):
        route([chip_at(n, 1) for n in range(g, g + group)])

    loads[5].wait()
    for c in range(2):
        for p in range(TILES):
            a = cour_in[c, pl.ds(p, levels, stride=ROWS), :]
            b = cour_in[c, pl.ds(p + TILES, levels, stride=ROWS), :]
            cour_t[c, p] = jnp.concatenate([a, b], axis=1)
    c_lon_out[0], c_lon_out[1] = pack_lon([cour_t[0, p] for p in range(TILES)])
    c_lat_out[0], c_lat_out[1] = pack_lat([cour_t[1, p] for p in range(TILES)])

    def edge_copies(lon_out, lon_in, lat_out, lat_in, send, recv):
        copies = []
        for i, step in enumerate((-1, 1)):
            copies.append(
                pltpu.make_async_remote_copy(
                    src_ref=lon_out.at[i],
                    dst_ref=lon_in.at[i],
                    send_sem=send.at[i],
                    recv_sem=recv.at[i],
                    device_id={"lev": lev_at(step)},
                    device_id_type=MESH,
                )
            )
        for i, step in enumerate((-1, 1)):
            copies.append(
                pltpu.make_async_remote_copy(
                    src_ref=lat_out.at[i],
                    dst_ref=lat_in.at[i],
                    send_sem=send.at[2 + i],
                    recv_sem=recv.at[2 + i],
                    device_id={"lat": lat_at(step)},
                    device_id_type=MESH,
                )
            )
        return copies

    c_copies = edge_copies(c_lon_out, c_lon_in, c_lat_out, c_lat_in, c_send, c_recv)

    def block(i):
        return pl.ds(pl.multiple_of(i * 16, 16), 16)

    def fwd_copy(t, d):
        return pltpu.make_async_remote_copy(
            src_ref=fwd_out.at[t, block(lev_at(d)), :],
            dst_ref=fwd_in.at[t, block(lev), :],
            send_sem=fwd_send.at[t, d],
            recv_sem=fwd_recv.at[t, d],
            device_id={"lev": lev_at(d)},
            device_id_type=MESH,
        )

    def start_fwd(t):
        def step(i, _):
            fwd_copy(t, far(i)).start()
            return _

        lax.fori_loop(0, n_lev - 1, step, 0)

    def msg_copy(n, change):
        target = 2 * chip_at(n, 1) + lax.rem(core + change, 2)
        return pltpu.make_async_remote_copy(
            src_ref=msg_out.at[target],
            dst_ref=msg_in.at[lat],
            send_sem=msg_send.at[2 * n + change],
            recv_sem=msg_recv.at[2 * n + change],
            device_id={"lat": target},
            device_id_type=MESH,
        )

    def others(n):
        return (1,) if chips[n] == (0, 0) else (0, 1)


    pl.semaphore_wait(barrier, n_lev + n_lat - 2)

    start_fwd(0)
    for n in range(len(chips)):
        for change in others(n):
            msg_copy(n, change).start()
    start_fwd(1)
    for copy in c_copies:
        copy.start()
    for t in range(2):
        fwd_in[t, block(lev), :] = fwd_out[t, block(lev), :]
    msg_in[lat] = msg_out[lat]


    loads[6].wait()
    loads[7].wait()
    for g in range(mat_in.shape[0] // 2):
        wide = []
        for odd in range(2):
            high, low = split(jnp.transpose(mat_in[2 * g + odd]))
            wide += [high, high, low]
        mix[pl.ds(g * levels, levels), :] = jnp.concatenate(wide, axis=1)
    tops = jnp.concatenate([top_in[0:8, :], top_in[8:16, :]], axis=1)


    columns = TILES * 128

    def arrive(n):
        m = chip_at(n, -1)
        one, two = pair(msg_in[2 * m], msg_in[2 * m + 1])
        kern_rows[n, 0:levels, :] = one
        kern_rows[n, levels : 2 * levels, :] = two

        def small_row(rows, first):
            third = lanes((1, 128)) % HALF // 16
            out = jnp.zeros((1, 128), F32)
            for i in range(3):
                moved = turn(rows[:SMALL], 16 * i - USED)
                out = jnp.where(third == i, moved[first + i : first + i + 1], out)
            return out

        wk = jnp.concatenate([one * small_row(one, 0), two * small_row(two, 0)], axis=0)
        at = pl.ds(n * 128, 128)
        high, low = split(wk)
        weighted[0 : 2 * levels, at] = high
        weighted[2 * levels :, at] = low
        target = small_row(one, 3).astype(I32) - 1
        hot[:, at] = one_hot(lax.broadcasted_iota(I32, (columns, 128), 0) == target)


    group = max(1, len(chips) // 2)
    for g in range(len(chips) // group):
        for n in range(g * group, (g + 1) * group):
            for change in others(n):
                msg_copy(n, change).wait()
        for n in range(g * group, (g + 1) * group):
            arrive(n)
        taken = pl.ds(g * group * 128, group * 128)
        for q in range(TILES // 2):
            got = dot(weighted[:, taken], hot[pl.ds(q * 256, 256), taken], (1, 1))
            got = got[: 2 * levels] + got[2 * levels :]
            for t in range(2):
                for i in range(2):
                    part = got[t * levels : (t + 1) * levels, i * 128 : (i + 1) * 128]
                    if g > 0:
                        part = part + deposit[t, 2 * q + i]
                    deposit[t, 2 * q + i] = part


    def wait_fwd(t):
        for i in range(n_lev - 1):
            fwd_copy(t, far(i)).wait()

    a_copies = []
    for t in range(2):
        wait_fwd(t)
        for q in range(TILES // 2):
            x = jnp.concatenate(
                [
                    fwd_in[t, pl.ds(p, levels, stride=TILES), :] + deposit[t, p]
                    for p in (2 * q, 2 * q + 1)
                ],
                axis=1,
            )
            top = jnp.concatenate([tops[2 * q : 2 * q + 1], tops[2 * q + 1 : 2 * q + 2]], axis=1)
            stack = []
            for odd in range(2):
                high, low = split(jnp.where(top % 2 == odd, x, 0.0))
                stack += [high, low, high]
            mixed = dot(mix[...], jnp.concatenate(stack, axis=0))
            result = mixed[0:levels]
            for g in range(1, mat_in.shape[0] // 2):
                result = jnp.where(top // 2 == g, mixed[g * levels : (g + 1) * levels], result)
            high, low = split(result)
            conv_split[pl.ds(t * levels, levels), pl.ds(q * 256, 256)] = high
            conv_split[pl.ds((2 + t) * levels, levels), pl.ds(q * 256, 256)] = low
            conv[t, 2 * q] = result[:, :128]
            conv[t, 2 * q + 1] = result[:, 128:]
        tiles = [conv[t, p] for p in range(TILES)]
        a_lon_out[t, 0], a_lon_out[t, 1] = pack_lon(tiles)
        a_lat_out[t, 0], a_lat_out[t, 1] = pack_lat(tiles)
        a_copies.append(
            edge_copies(
                a_lon_out.at[t],
                a_lon_in.at[t],
                a_lat_out.at[t],
                a_lat_in.at[t],
                a_send.at[t],
                a_recv.at[t],
            )
        )
        for copy in a_copies[t]:
            copy.start()

    first, last = lat == 0, lat == n_lat - 1
    for copy in c_copies:
        copy.wait()
    from_east, from_west = unfold(c_lon_in[0], levels), unfold(c_lon_in[1], levels)
    from_north, from_south = c_lat_in[0], c_lat_in[1]
    from_north = jnp.where(last, 0.0, from_north)
    from_south = jnp.where(first, 0.0, from_south)
    rows_c = [cour_t[1, p] for p in range(TILES)]
    rows_c[0] = jnp.where(low_half(rows_c[0].shape) & first, 0.0, rows_c[0])
    rows_c = extend_lat(rows_c, from_south, from_north)
    for p in range(TILES):
        here = cour_t[0, p]
        before_x, after_x, after2_x = shift_lon(here, p, from_west, from_east, (-1, 1, 2))
        lon_w = face_weights(before_x, here, after_x, after2_x)
        lat_w = face_weights(rows_c[p + 1], rows_c[p + 2], rows_c[p + 3], rows_c[p + 4])
        weights[p, 0] = 1.0 + lon_w[2] + lat_w[2]
        for i, j in enumerate((0, 1, 3, 4)):
            weights[p, 1 + i] = lon_w[j]
            weights[p, 5 + i] = lat_w[j]


    def back_copy(t, d):
        return pltpu.make_async_remote_copy(
            src_ref=back_out.at[t, block(lev_at(d)), :],
            dst_ref=back_in.at[t, block(lev), :],
            send_sem=back_send.at[t, d],
            recv_sem=back_recv.at[t, d],
            device_id={"lev": lev_at(d)},
            device_id_type=MESH,
        )

    keeps = []
    for t in range(2):
        for copy in a_copies[t]:
            copy.wait()
        from_east, from_west = (unfold(a_lon_in[t, i], levels) for i in range(2))
        from_north, from_south = a_lat_in[t, 0], a_lat_in[t, 1]
        from_north = jnp.where(last, 0.0, from_north)
        from_south = jnp.where(first, 0.0, from_south)
        tiles = extend_lat([conv[t, p] for p in range(TILES)], from_south, from_north)
        for p in range(TILES):
            here = tiles[p + 2]
            around = shift_lon(here, p, from_west, from_east, (-2, -1, 1, 2))
            around += [tiles[p], tiles[p + 1], tiles[p + 3], tiles[p + 4]]
            total = weights[p, 0] * here
            for i in range(8):
                total = total + weights[p, 1 + i] * around[i]
            back_out[t, pl.ds(p, levels, stride=TILES), :] = total

        def start_back(i, _, t=t):
            back_copy(t, far(i)).start()
            return _

        lax.fori_loop(0, n_lev - 1, start_back, 0)
        keeps.append(
            pltpu.make_async_copy(
                back_out.at[t, block(lev), :], back_in.at[t, block(lev), :], keep_sem.at[t]
            )
        )
        keeps[t].start()


    for m in range(n_lat // 4):
        picked = dot(conv_split[...], hot[:, pl.ds(m * 256, 256)])
        picked = picked[: 2 * levels] + picked[2 * levels :]
        for i in range(2):
            product = picked[:, i * 128 : (i + 1) * 128] * kern_rows[2 * m + i]
            sums = [
                jnp.sum(product[t * levels : (t + 1) * levels], axis=0, keepdims=True)
                for t in range(2)
            ]
            which = lax.broadcasted_iota(I32, (MSG, 128), 0)
            both = jnp.where(which == 0, sums[0], jnp.where(which == 1, sums[1], 0.0))
            ret_out[4 * m + 2 * i] = both
            ret_out[4 * m + 2 * i + 1] = turn(both, HALF)

    def ret_copy(n, change):
        other = lax.rem(core + change, 2)
        return pltpu.make_async_remote_copy(
            src_ref=ret_out.at[2 * n + other],
            dst_ref=ret_in.at[lat],
            send_sem=ret_send.at[2 * n + change],
            recv_sem=ret_recv.at[2 * n + change],
            device_id={"lat": 2 * chip_at(n, -1) + other},
            device_id_type=MESH,
        )


    for n in range(len(chips)):
        for change in others(n):
            ret_copy(n, change).start()
    ret_in[lat] = ret_out[core]
    for n in range(len(chips)):
        for change in others(n):
            ret_copy(n, change).wait()

    for m in range(n_lat // 2):
        both, _unused = pair(ret_in[2 * m], ret_in[2 * m + 1])
        ret_split[:, pl.ds(m * 128, 128)] = jnp.concatenate(split(both), axis=0)
    own = dot(ret_split[...], place[...])
    own = own[:MSG] + own[MSG:]
    sens[...] = own[0:2]
    sens_store = pltpu.make_async_copy(sens, sens_out, keep_sem.at[2])
    sens_store.start()


    for t in range(2):
        for i in range(n_lev - 1):
            back_copy(t, far(i)).wait()
        keeps[t].wait()
    sens_store.wait()


def finish(n_lev, back_hbm, sens_hbm, out_hbm, sens_out, back, out, load_sem, store_sem):
    loads, stores = [], []
    for t in range(2):
        loads.append(pltpu.make_async_copy(back_hbm.at[t], back.at[t], load_sem.at[t]))
        loads[t].start()
        stores.append(pltpu.make_async_copy(out.at[t], out_hbm.at[t], store_sem.at[t]))
    sens_copy = pltpu.make_async_copy(sens_hbm, sens_out, store_sem.at[2])
    sens_copy.start()
    for t in range(2):
        loads[t].wait()
        for m in range(n_lev // 2):
            for kk in range(2):
                a, b = pair(
                    back[t, pl.ds(m * 32 + kk * 8, 8), :],
                    back[t, pl.ds(m * 32 + 16 + kk * 8, 8), :],
                )
                out[t, kk, 0:8, pl.ds(m * 128, 128)] = a
                out[t, kk, 8:16, pl.ds(m * 128, 128)] = b
        stores[t].start()
    for store in stores:
        store.wait()
    sens_copy.wait()


def per_device(
    n_lev,
    n_lat,
    adjoint_in,
    courant,
    cloud_top,
    conv_inverse,
    sounding_kernel,
    sounding_weight,
    sounding_owner,
    sounding_cell,
    sounding_count,
):
    levels = 2 * n_lev
    slots = sounding_kernel.shape[2]
    classes = conv_inverse.shape[0]
    columns = TILES * 128
    spots = n_lat * HALF
    operands = (
        adjoint_in,
        courant.reshape(2, levels * ROWS, HALF),
        cloud_top,
        conv_inverse,
        sounding_kernel.reshape(slots, 2 * levels).T,
        sounding_weight.reshape(slots, 2).T,
        sounding_owner.reshape(1, slots),
        sounding_cell.reshape(1, slots),
        sounding_count,
    )
    vm, dma = pltpu.VMEM, pltpu.SemaphoreType.DMA
    scratch = [vm(x.shape, x.dtype) for x in operands[:-1]]
    scratch += [vm((2, n_lev * 16, 128), F32) for _ in range(3)]
    scratch += [vm((n_lat, levels, 128), F32) for _ in range(2)]
    scratch += [vm((n_lat, MSG, 128), F32) for _ in range(2)]
    scratch += [vm((2, 8, 128), F32) for _ in range(2)]
    scratch += [vm((2, levels, 128), F32) for _ in range(2)]
    scratch += [vm((2, 2, 8, 128), F32) for _ in range(2)]
    scratch += [vm((2, 2, levels, 128), F32) for _ in range(2)]
    scratch += [
        vm((spots, slots), BF16),
        vm((n_lat // 2, 2 * levels, 128), F32),
        vm((4 * levels, spots), BF16),
        vm((columns, spots), BF16),
        vm((2, TILES, levels, 128), F32),
        vm((2, TILES, levels, 128), F32),
        vm((TILES, 9, levels, 128), F32),
        vm((classes // 2 * levels, 6 * levels), BF16),
        vm((2, TILES, levels, 128), F32),
        vm((4 * levels, columns), BF16),
        vm((2 * MSG, spots), BF16),
        vm((2, slots), F32),
        dma((8,)),
        dma((3,)),
    ]
    scratch += [dma((2, n_lev)) for _ in range(4)]
    scratch += [dma((n_lat,)) for _ in range(4)]
    scratch += [dma((4,)) for _ in range(2)]
    scratch += [dma((2, 4)) for _ in range(2)]
    in_hbm = pl.BlockSpec(memory_space=pltpu.HBM)
    back, sens = pl.pallas_call(
        functools.partial(kernel, n_lev, n_lat),
        out_shape=(
            jax.ShapeDtypeStruct((2, n_lev * 16, 128), F32),
            jax.ShapeDtypeStruct((2, slots), F32),
        ),
        in_specs=[in_hbm] * (len(operands) - 1) + [pl.BlockSpec(memory_space=pltpu.SMEM)],
        out_specs=(in_hbm, in_hbm),
        scratch_shapes=scratch,
        compiler_params=pltpu.CompilerParams(
            collective_id=0, has_side_effects=True, vmem_limit_bytes=60 * 2**20
        ),
    )(*operands)
    out, sens = pl.pallas_call(
        functools.partial(finish, n_lev),
        out_shape=(
            jax.ShapeDtypeStruct(adjoint_in.shape, F32),
            jax.ShapeDtypeStruct((2, slots), F32),
        ),
        in_specs=[in_hbm] * 2,
        out_specs=(in_hbm, in_hbm),
        scratch_shapes=[
            vm((2, n_lev * 16, 128), F32),
            vm(adjoint_in.shape, F32),
            dma((2,)),
            dma((3,)),
        ],
        compiler_params=pltpu.CompilerParams(vmem_limit_bytes=60 * 2**20),
    )(back, sens)
    return out, sens.T.reshape(1, 1, slots, 2)


def solution(mesh):
    placed = (
        P(None, "lev", "lat", None),
        P(None, None, "lat", "lev"),
        P("lat", "lev"),
        P(),
        P("lev", "lat", None, None),
        P("lev", "lat", None, None),
        P("lev", "lat", None),
        P("lev", "lat", None),
        P("lev", "lat"),
    )
    return jax.shard_map(
        functools.partial(per_device, mesh.shape["lev"], mesh.shape["lat"]),
        mesh=mesh,
        in_specs=placed,
        out_specs=(P(None, "lev", "lat", None), P("lev", "lat", None, None)),
        check_vma=False,
    )
```

```python
import functools

import jax
import jax.numpy as jnp
from jax import lax
from jax.experimental import pallas as pl
from jax.experimental.pallas import tpu as pltpu
from jax.sharding import PartitionSpec as P

MESH = pl.DeviceIdType.MESH
F32, BF16, I32 = jnp.float32, jnp.bfloat16, jnp.int32
ROWS = 16
TILES = 8
HALF = 64
USED = 48
SMALL = 8
MSG = 8
CHUNKS = 2


def lanes(shape):
    return lax.broadcasted_iota(I32, shape, len(shape) - 1)


def turn(x, shift):
    shift = shift % 128
    return x if shift == 0 else pltpu.roll(x, shift, x.ndim - 1)


def low_half(shape):
    return lanes(shape) < HALF


def pair(a, b):
    low = low_half(a.shape)
    return jnp.where(low, a, turn(b, HALF)), jnp.where(low, turn(a, HALF), b)


def split(x):
    high = x.astype(BF16)
    return high, (x - high.astype(F32)).astype(BF16)


def dot(a, b, contract=(1, 0)):
    return lax.dot_general(
        a, b, (((contract[0],), (contract[1],)), ((), ())), preferred_element_type=F32
    )


def one_hot(mask):
    return jnp.where(mask, 1.0, 0.0).astype(BF16)


def pack_lon(tiles):
    x = lanes(tiles[0].shape) % HALF
    to_west, to_east = tiles[0], turn(tiles[0], 66)
    for p in range(1, TILES):
        here = x // 2 == p
        to_west = jnp.where(here, turn(tiles[p], 2 * p), to_west)
        to_east = jnp.where(here, turn(tiles[p], 2 * p + 66), to_east)
    return tuple(fold(edge) for edge in (to_west, to_east))


def fold(edge):
    out = edge[0:8]
    for i in range(1, edge.shape[0] // 8):
        here = lanes(out.shape) % HALF // 16 == i
        out = jnp.where(here, turn(edge[8 * i : 8 * i + 8], 16 * i), out)
    return out


def unfold(edge, levels):
    return jnp.concatenate([turn(edge, -16 * i) for i in range(levels // 8)], axis=0)


def shift_lon(tile, p, from_west, from_east, steps):
    x = lanes(tile.shape) % HALF
    east = turn(from_east, HALF - 2 * p)
    west = turn(from_west, 126 - 2 * p)
    out = []
    for d in steps:
        if d > 0:
            out.append(turn(jnp.where(x < d, east, tile), -d))
        else:
            out.append(turn(jnp.where(x >= HALF + d, west, tile), -d))
    return out


def pack_lat(tiles):
    low = low_half(tiles[0].shape)
    to_south = jnp.where(low, tiles[0], turn(tiles[1], HALF))
    to_north = jnp.where(low, turn(tiles[6], HALF), tiles[7])
    return to_south, to_north


def extend_lat(tiles, from_south, from_north):
    low = low_half(tiles[0].shape)
    return (
        [
            jnp.where(low, from_south, turn(tiles[6], HALF)),
            turn(jnp.where(low, tiles[7], from_south), HALF),
        ]
        + list(tiles)
        + [
            turn(jnp.where(low, from_north, tiles[0]), HALF),
            jnp.where(low, turn(tiles[1], HALF), from_north),
        ]
    )


def face_weights(before, here, after, after2):
    def parts(c):
        pos, neg = jnp.maximum(c, 0.0), jnp.minimum(c, 0.0)
        return pos, neg, 0.25 * pos * (1.0 - pos), 0.25 * neg * (1.0 + neg)

    _, _, _, sn_before = parts(before)
    _, neg_here, sp_here, _ = parts(here)
    pos_after, _, _, sn_after = parts(after)
    _, _, sp_after2, _ = parts(after2)
    own = neg_here + sp_here
    nxt = pos_after + sn_after
    return sn_before, -own - sn_before, own - nxt, nxt + sp_after2, -sp_after2


def kernel(
    n_lev,
    n_lat,
    adj_hbm,
    cour_hbm,
    top_hbm,
    mat_hbm,
    kern_hbm,
    wt_hbm,
    owner_hbm,
    cell_hbm,
    count_ref,
    back_in,
    sens_out,
    adj_in,
    cour_in,
    top_in,
    mat_in,
    kern_in,
    wt_in,
    owner_in,
    cell_in,
    fwd_out,
    fwd_in,
    back_out,
    msg_out,
    msg_in,
    ret_out,
    ret_in,
    c_lon_out,
    c_lon_in,
    c_lat_out,
    c_lat_in,
    a_lon_out,
    a_lon_in,
    a_lat_out,
    a_lat_in,
    place,
    kern_rows,
    weighted,
    hot,
    deposit,
    cour_t,
    weights,
    mix,
    conv,
    conv_split,
    ret_split,
    sens,
    in_sem,
    keep_sem,
    fwd_send,
    fwd_recv,
    back_send,
    back_recv,
    msg_send,
    msg_recv,
    ret_send,
    ret_recv,
    c_send,
    c_recv,
    a_send,
    a_recv,
):
    lev, lat = lax.axis_index("lev"), lax.axis_index("lat")
    levels = 2 * n_lev
    slots = owner_in.shape[1]

    def lev_at(d):
        return lax.rem(lev + d + n_lev, n_lev)

    def lat_at(d):
        return lax.rem(lat + d + n_lat, n_lat)

    n_y = max(2, n_lat // 8)
    n_x = n_lat // (2 * n_y)
    at_x, at_y, core = lat // (2 * n_y), lax.rem(lat // 2, n_y), lax.rem(lat, 2)

    def hops(step):
        return min(step[0], n_x - step[0]) + min(step[1], n_y - step[1])

    chips = sorted(((i, j) for i in range(n_x) for j in range(n_y)), key=hops)

    def chip_at(n, sign):
        i, j = chips[n]
        return lax.rem(at_x + sign * i + n_x, n_x) * n_y + lax.rem(at_y + sign * j + n_y, n_y)

    def far(i):
        half = (i + 1) // 2
        return n_lev // 2 + half * (1 - 2 * (i % 2))

    loads = [
        pltpu.make_async_copy(source, target, in_sem.at[i])
        for i, (source, target) in enumerate(
            [
                (adj_hbm, adj_in),
                (owner_hbm, owner_in),
                (cell_hbm, cell_in),
                (kern_hbm, kern_in),
                (wt_hbm, wt_in),
                (cour_hbm, cour_in),
                (top_hbm, top_in),
                (mat_hbm, mat_in),
            ]
        )
    ]
    for load in loads:
        load.start()

    barrier = pltpu.get_barrier_semaphore()

    def greet_lev(d, _):
        pl.semaphore_signal(barrier, inc=1, device_id={"lev": lev_at(far(d))}, device_id_type=MESH)
        return _

    def greet_lat(d, _):
        pl.semaphore_signal(barrier, inc=1, device_id={"lat": lat_at(d)}, device_id_type=MESH)
        return _

    lax.fori_loop(0, n_lev - 1, greet_lev, 0)
    lax.fori_loop(1, n_lat, greet_lat, 0)

    loads[0].wait()
    for t in range(2):
        for m in range(n_lev // 2):
            for kk in range(2):
                cols = pl.ds(m * 128, 128)
                a, b = pair(adj_in[t, kk, 0:8, cols], adj_in[t, kk, 8:16, cols])
                fwd_out[t, pl.ds(m * 32 + kk * 8, 8), :] = a
                fwd_out[t, pl.ds(m * 32 + 16 + kk * 8, 8), :] = b
    for i in range(1, 5):
        loads[i].wait()
    owner, cell = owner_in[...], cell_in[...]
    valid = lanes((1, slots)) < count_ref[0, 0]
    owned = (lax.broadcasted_iota(I32, (n_lat, slots), 0) == owner) & valid
    upper = one_hot(lax.broadcasted_iota(I32, (slots, slots), 0) < lanes((slots, slots)))
    before = dot(one_hot(owned), upper)
    rank = jnp.sum(jnp.where(owned, before, 0.0), axis=0, keepdims=True).astype(I32)
    slot = jnp.where(valid, owner * HALF + rank, -1)
    row = cell // HALF
    packed = (row % TILES) * 128 + (row // TILES) * HALF + cell % HALF
    which = lax.broadcasted_iota(I32, (2 * SMALL, slots), 0)
    small = jnp.where((which >= 3) & (which < 6), (packed + 1).astype(F32), 0.0)
    small = jnp.where(which < 3, wt_in[0:1, :], small)
    small = jnp.where((which >= SMALL) & (which < SMALL + 3), wt_in[1:2, :], small)
    table = jnp.concatenate([kern_in[...], small], axis=0)
    tall = 2 * levels + 2 * SMALL
    table = jnp.concatenate(split(table), axis=0)

    def route(chips_m):
        hits = []
        for m in chips_m:
            base = pl.multiple_of(m * 128, 128)
            spot = lax.broadcasted_iota(I32, (128, slots), 0) + base
            hits.append(one_hot(spot == slot))
            place[pl.ds(base, 128), :] = hits[-1]
        sent = dot(table, jnp.concatenate(hits, axis=0), (1, 1))
        sent = sent[:tall] + sent[tall:]
        for i, m in enumerate(chips_m):
            part = sent[:, i * 128 : (i + 1) * 128]
            t0 = jnp.concatenate([part[:levels], part[2 * levels : 2 * levels + SMALL]], axis=0)
            t1 = jnp.concatenate(
                [part[levels : 2 * levels], part[2 * levels + SMALL :]], axis=0
            )
            for change, full in enumerate(pair(t0, t1)):
                rest = full[levels:]
                third = lax.broadcasted_iota(I32, rest.shape, 0) % 3
                moved = jnp.where(third == 1, turn(rest, 32), turn(rest, 16))
                moved = jnp.where(third == 0, turn(rest, 48), moved)
                free = lanes(rest.shape) % HALF >= USED
                msg_out[2 * m + change, 0:SMALL, :] = jnp.where(free, moved, full[:SMALL])
                if levels > SMALL:
                    msg_out[2 * m + change, SMALL:levels, :] = full[SMALL:levels]

    group = max(1, len(chips) // 4)
    for g in range(0, len(chips), group):
        route([chip_at(n, 1) for n in range(g, g + group)])

    loads[5].wait()
    for c in range(2):
        for p in range(TILES):
            a = cour_in[c, pl.ds(p, levels, stride=ROWS), :]
            b = cour_in[c, pl.ds(p + TILES, levels, stride=ROWS), :]
            cour_t[c, p] = jnp.concatenate([a, b], axis=1)
    c_lon_out[0], c_lon_out[1] = pack_lon([cour_t[0, p] for p in range(TILES)])
    c_lat_out[0], c_lat_out[1] = pack_lat([cour_t[1, p] for p in range(TILES)])

    def edge_copies(lon_out, lon_in, lat_out, lat_in, send, recv):
        copies = []
        for i, step in enumerate((-1, 1)):
            copies.append(
                pltpu.make_async_remote_copy(
                    src_ref=lon_out.at[i],
                    dst_ref=lon_in.at[i],
                    send_sem=send.at[i],
                    recv_sem=recv.at[i],
                    device_id={"lev": lev_at(step)},
                    device_id_type=MESH,
                )
            )
        for i, step in enumerate((-1, 1)):
            copies.append(
                pltpu.make_async_remote_copy(
                    src_ref=lat_out.at[i],
                    dst_ref=lat_in.at[i],
                    send_sem=send.at[2 + i],
                    recv_sem=recv.at[2 + i],
                    device_id={"lat": lat_at(step)},
                    device_id_type=MESH,
                )
            )
        return copies

    c_copies = edge_copies(c_lon_out, c_lon_in, c_lat_out, c_lat_in, c_send, c_recv)

    def block(i):
        return pl.ds(pl.multiple_of(i * 16, 16), 16)

    def fwd_copy(t, d):
        return pltpu.make_async_remote_copy(
            src_ref=fwd_out.at[t, block(lev_at(d)), :],
            dst_ref=fwd_in.at[t, block(lev), :],
            send_sem=fwd_send.at[t, d],
            recv_sem=fwd_recv.at[t, d],
            device_id={"lev": lev_at(d)},
            device_id_type=MESH,
        )

    def start_fwd(t):
        def step(i, _):
            fwd_copy(t, far(i)).start()
            return _

        lax.fori_loop(0, n_lev - 1, step, 0)

    def msg_copy(n, change):
        target = 2 * chip_at(n, 1) + lax.rem(core + change, 2)
        return pltpu.make_async_remote_copy(
            src_ref=msg_out.at[target],
            dst_ref=msg_in.at[lat],
            send_sem=msg_send.at[2 * n + change],
            recv_sem=msg_recv.at[2 * n + change],
            device_id={"lat": target},
            device_id_type=MESH,
        )

    def others(n):
        return (1,) if chips[n] == (0, 0) else (0, 1)


    pl.semaphore_wait(barrier, n_lev + n_lat - 2)

    start_fwd(0)
    for n in range(len(chips)):
        for change in others(n):
            msg_copy(n, change).start()
    start_fwd(1)
    for copy in c_copies:
        copy.start()
    for t in range(2):
        fwd_in[t, block(lev), :] = fwd_out[t, block(lev), :]
    msg_in[lat] = msg_out[lat]


    loads[6].wait()
    loads[7].wait()
    for g in range(mat_in.shape[0] // 2):
        wide = []
        for odd in range(2):
            high, low = split(jnp.transpose(mat_in[2 * g + odd]))
            wide += [high, high, low]
        mix[pl.ds(g * levels, levels), :] = jnp.concatenate(wide, axis=1)
    tops = jnp.concatenate([top_in[0:8, :], top_in[8:16, :]], axis=1)


    columns = TILES * 128

    def arrive(n):
        m = chip_at(n, -1)
        one, two = pair(msg_in[2 * m], msg_in[2 * m + 1])
        kern_rows[n, 0:levels, :] = one
        kern_rows[n, levels : 2 * levels, :] = two

        def small_row(rows, first):
            third = lanes((1, 128)) % HALF // 16
            out = jnp.zeros((1, 128), F32)
            for i in range(3):
                moved = turn(rows[:SMALL], 16 * i - USED)
                out = jnp.where(third == i, moved[first + i : first + i + 1], out)
            return out

        wk = jnp.concatenate([one * small_row(one, 0), two * small_row(two, 0)], axis=0)
        at = pl.ds(n * 128, 128)
        high, low = split(wk)
        weighted[0 : 2 * levels, at] = high
        weighted[2 * levels :, at] = low
        target = small_row(one, 3).astype(I32) - 1
        hot[:, at] = one_hot(lax.broadcasted_iota(I32, (columns, 128), 0) == target)


    group = max(1, len(chips) // 2)
    for g in range(len(chips) // group):
        for n in range(g * group, (g + 1) * group):
            for change in others(n):
                msg_copy(n, change).wait()
        for n in range(g * group, (g + 1) * group):
            arrive(n)
        taken = pl.ds(g * group * 128, group * 128)
        for q in range(TILES // 2):
            got = dot(weighted[:, taken], hot[pl.ds(q * 256, 256), taken], (1, 1))
            got = got[: 2 * levels] + got[2 * levels :]
            for t in range(2):
                for i in range(2):
                    part = got[t * levels : (t + 1) * levels, i * 128 : (i + 1) * 128]
                    if g > 0:
                        part = part + deposit[t, 2 * q + i]
                    deposit[t, 2 * q + i] = part


    def wait_fwd(t):
        for i in range(n_lev - 1):
            fwd_copy(t, far(i)).wait()

    a_copies = []
    for t in range(2):
        wait_fwd(t)
        for q in range(TILES // 2):
            x = jnp.concatenate(
                [
                    fwd_in[t, pl.ds(p, levels, stride=TILES), :] + deposit[t, p]
                    for p in (2 * q, 2 * q + 1)
                ],
                axis=1,
            )
            top = jnp.concatenate([tops[2 * q : 2 * q + 1], tops[2 * q + 1 : 2 * q + 2]], axis=1)
            stack = []
            for odd in range(2):
                high, low = split(jnp.where(top % 2 == odd, x, 0.0))
                stack += [high, low, high]
            mixed = dot(mix[...], jnp.concatenate(stack, axis=0))
            result = mixed[0:levels]
            for g in range(1, mat_in.shape[0] // 2):
                result = jnp.where(top // 2 == g, mixed[g * levels : (g + 1) * levels], result)
            high, low = split(result)
            conv_split[pl.ds(t * levels, levels), pl.ds(q * 256, 256)] = high
            conv_split[pl.ds((2 + t) * levels, levels), pl.ds(q * 256, 256)] = low
            conv[t, 2 * q] = result[:, :128]
            conv[t, 2 * q + 1] = result[:, 128:]
        tiles = [conv[t, p] for p in range(TILES)]
        a_lon_out[t, 0], a_lon_out[t, 1] = pack_lon(tiles)
        a_lat_out[t, 0], a_lat_out[t, 1] = pack_lat(tiles)
        a_copies.append(
            edge_copies(
                a_lon_out.at[t],
                a_lon_in.at[t],
                a_lat_out.at[t],
                a_lat_in.at[t],
                a_send.at[t],
                a_recv.at[t],
            )
        )
        for copy in a_copies[t]:
            copy.start()

    first, last = lat == 0, lat == n_lat - 1
    for copy in c_copies:
        copy.wait()
    from_east, from_west = unfold(c_lon_in[0], levels), unfold(c_lon_in[1], levels)
    from_north, from_south = c_lat_in[0], c_lat_in[1]
    from_north = jnp.where(last, 0.0, from_north)
    from_south = jnp.where(first, 0.0, from_south)
    rows_c = [cour_t[1, p] for p in range(TILES)]
    rows_c[0] = jnp.where(low_half(rows_c[0].shape) & first, 0.0, rows_c[0])
    rows_c = extend_lat(rows_c, from_south, from_north)
    for p in range(TILES):
        here = cour_t[0, p]
        before_x, after_x, after2_x = shift_lon(here, p, from_west, from_east, (-1, 1, 2))
        lon_w = face_weights(before_x, here, after_x, after2_x)
        lat_w = face_weights(rows_c[p + 1], rows_c[p + 2], rows_c[p + 3], rows_c[p + 4])
        weights[p, 0] = 1.0 + lon_w[2] + lat_w[2]
        for i, j in enumerate((0, 1, 3, 4)):
            weights[p, 1 + i] = lon_w[j]
            weights[p, 5 + i] = lat_w[j]


    def back_copy(t, d):
        return pltpu.make_async_remote_copy(
            src_ref=back_out.at[t, block(lev_at(d)), :],
            dst_ref=back_in.at[t, block(lev), :],
            send_sem=back_send.at[t, d],
            recv_sem=back_recv.at[t, d],
            device_id={"lev": lev_at(d)},
            device_id_type=MESH,
        )

    keeps = []
    for t in range(2):
        for copy in a_copies[t]:
            copy.wait()
        from_east, from_west = (unfold(a_lon_in[t, i], levels) for i in range(2))
        from_north, from_south = a_lat_in[t, 0], a_lat_in[t, 1]
        from_north = jnp.where(last, 0.0, from_north)
        from_south = jnp.where(first, 0.0, from_south)
        tiles = extend_lat([conv[t, p] for p in range(TILES)], from_south, from_north)
        for p in range(TILES):
            here = tiles[p + 2]
            around = shift_lon(here, p, from_west, from_east, (-2, -1, 1, 2))
            around += [tiles[p], tiles[p + 1], tiles[p + 3], tiles[p + 4]]
            total = weights[p, 0] * here
            for i in range(8):
                total = total + weights[p, 1 + i] * around[i]
            back_out[t, pl.ds(p, levels, stride=TILES), :] = total

        def start_back(i, _, t=t):
            back_copy(t, far(i)).start()
            return _

        lax.fori_loop(0, n_lev - 1, start_back, 0)
        keeps.append(
            pltpu.make_async_copy(
                back_out.at[t, block(lev), :], back_in.at[t, block(lev), :], keep_sem.at[t]
            )
        )
        keeps[t].start()


    for m in range(n_lat // 4):
        picked = dot(conv_split[...], hot[:, pl.ds(m * 256, 256)])
        picked = picked[: 2 * levels] + picked[2 * levels :]
        for i in range(2):
            product = picked[:, i * 128 : (i + 1) * 128] * kern_rows[2 * m + i]
            sums = [
                jnp.sum(product[t * levels : (t + 1) * levels], axis=0, keepdims=True)
                for t in range(2)
            ]
            which = lax.broadcasted_iota(I32, (MSG, 128), 0)
            both = jnp.where(which == 0, sums[0], jnp.where(which == 1, sums[1], 0.0))
            ret_out[4 * m + 2 * i] = both
            ret_out[4 * m + 2 * i + 1] = turn(both, HALF)

    def ret_copy(n, change):
        other = lax.rem(core + change, 2)
        return pltpu.make_async_remote_copy(
            src_ref=ret_out.at[2 * n + other],
            dst_ref=ret_in.at[lat],
            send_sem=ret_send.at[2 * n + change],
            recv_sem=ret_recv.at[2 * n + change],
            device_id={"lat": 2 * chip_at(n, -1) + other},
            device_id_type=MESH,
        )


    for n in range(len(chips)):
        for change in others(n):
            ret_copy(n, change).start()
    ret_in[lat] = ret_out[core]
    for n in range(len(chips)):
        for change in others(n):
            ret_copy(n, change).wait()

    for m in range(n_lat // 2):
        both, _unused = pair(ret_in[2 * m], ret_in[2 * m + 1])
        ret_split[:, pl.ds(m * 128, 128)] = jnp.concatenate(split(both), axis=0)
    own = dot(ret_split[...], place[...])
    own = own[:MSG] + own[MSG:]
    sens[...] = own[0:2]
    sens_store = pltpu.make_async_copy(sens, sens_out, keep_sem.at[2])
    sens_store.start()


    for t in range(2):
        for i in range(n_lev - 1):
            back_copy(t, far(i)).wait()
        keeps[t].wait()
    sens_store.wait()


def finish(n_lev, back_hbm, sens_hbm, out_hbm, sens_out, back, out, load_sem, store_sem):
    pairs = n_lev // 2
    wide = max(1, pairs // CHUNKS)
    sens_copy = pltpu.make_async_copy(sens_hbm, sens_out, store_sem.at[2 * CHUNKS])
    loads, stores = [], []
    for t in range(2):
        for c in range(pairs // wide):
            rows, cols = pl.ds(c * wide * 32, wide * 32), pl.ds(c * wide * 128, wide * 128)
            i = t * CHUNKS + c
            loads.append(
                pltpu.make_async_copy(
                    back_hbm.at[t, rows, :], back.at[t, rows, :], load_sem.at[i]
                )
            )
            stores.append(
                pltpu.make_async_copy(
                    out.at[t, :, :, cols], out_hbm.at[t, :, :, cols], store_sem.at[i]
                )
            )
    for load in loads:
        load.start()
    sens_copy.start()
    for i, (load, store) in enumerate(zip(loads, stores)):
        t, c = i // (pairs // wide), i % (pairs // wide)
        load.wait()
        for m in range(c * wide, (c + 1) * wide):
            for kk in range(2):
                a, b = pair(
                    back[t, pl.ds(m * 32 + kk * 8, 8), :],
                    back[t, pl.ds(m * 32 + 16 + kk * 8, 8), :],
                )
                out[t, kk, 0:8, pl.ds(m * 128, 128)] = a
                out[t, kk, 8:16, pl.ds(m * 128, 128)] = b
        store.start()
    for store in stores:
        store.wait()
    sens_copy.wait()


def per_device(
    n_lev,
    n_lat,
    adjoint_in,
    courant,
    cloud_top,
    conv_inverse,
    sounding_kernel,
    sounding_weight,
    sounding_owner,
    sounding_cell,
    sounding_count,
):
    levels = 2 * n_lev
    slots = sounding_kernel.shape[2]
    classes = conv_inverse.shape[0]
    columns = TILES * 128
    spots = n_lat * HALF
    operands = (
        adjoint_in,
        courant.reshape(2, levels * ROWS, HALF),
        cloud_top,
        conv_inverse,
        sounding_kernel.reshape(slots, 2 * levels).T,
        sounding_weight.reshape(slots, 2).T,
        sounding_owner.reshape(1, slots),
        sounding_cell.reshape(1, slots),
        sounding_count,
    )
    vm, dma = pltpu.VMEM, pltpu.SemaphoreType.DMA
    scratch = [vm(x.shape, x.dtype) for x in operands[:-1]]
    scratch += [vm((2, n_lev * 16, 128), F32) for _ in range(3)]
    scratch += [vm((n_lat, levels, 128), F32) for _ in range(2)]
    scratch += [vm((n_lat, MSG, 128), F32) for _ in range(2)]
    scratch += [vm((2, 8, 128), F32) for _ in range(2)]
    scratch += [vm((2, levels, 128), F32) for _ in range(2)]
    scratch += [vm((2, 2, 8, 128), F32) for _ in range(2)]
    scratch += [vm((2, 2, levels, 128), F32) for _ in range(2)]
    scratch += [
        vm((spots, slots), BF16),
        vm((n_lat // 2, 2 * levels, 128), F32),
        vm((4 * levels, spots), BF16),
        vm((columns, spots), BF16),
        vm((2, TILES, levels, 128), F32),
        vm((2, TILES, levels, 128), F32),
        vm((TILES, 9, levels, 128), F32),
        vm((classes // 2 * levels, 6 * levels), BF16),
        vm((2, TILES, levels, 128), F32),
        vm((4 * levels, columns), BF16),
        vm((2 * MSG, spots), BF16),
        vm((2, slots), F32),
        dma((8,)),
        dma((3,)),
    ]
    scratch += [dma((2, n_lev)) for _ in range(4)]
    scratch += [dma((n_lat,)) for _ in range(4)]
    scratch += [dma((4,)) for _ in range(2)]
    scratch += [dma((2, 4)) for _ in range(2)]
    in_hbm = pl.BlockSpec(memory_space=pltpu.HBM)
    back, sens = pl.pallas_call(
        functools.partial(kernel, n_lev, n_lat),
        out_shape=(
            jax.ShapeDtypeStruct((2, n_lev * 16, 128), F32),
            jax.ShapeDtypeStruct((2, slots), F32),
        ),
        in_specs=[in_hbm] * (len(operands) - 1) + [pl.BlockSpec(memory_space=pltpu.SMEM)],
        out_specs=(in_hbm, in_hbm),
        scratch_shapes=scratch,
        compiler_params=pltpu.CompilerParams(
            collective_id=0, has_side_effects=True, vmem_limit_bytes=60 * 2**20
        ),
    )(*operands)
    out, sens = pl.pallas_call(
        functools.partial(finish, n_lev),
        out_shape=(
            jax.ShapeDtypeStruct(adjoint_in.shape, F32),
            jax.ShapeDtypeStruct((2, slots), F32),
        ),
        in_specs=[in_hbm] * 2,
        out_specs=(in_hbm, in_hbm),
        scratch_shapes=[
            vm((2, n_lev * 16, 128), F32),
            vm(adjoint_in.shape, F32),
            dma((2 * CHUNKS,)),
            dma((2 * CHUNKS + 1,)),
        ],
        compiler_params=pltpu.CompilerParams(vmem_limit_bytes=60 * 2**20),
    )(back, sens)
    return out, sens.T.reshape(1, 1, slots, 2)


def solution(mesh):
    placed = (
        P(None, "lev", "lat", None),
        P(None, None, "lat", "lev"),
        P("lat", "lev"),
        P(),
        P("lev", "lat", None, None),
        P("lev", "lat", None, None),
        P("lev", "lat", None),
        P("lev", "lat", None),
        P("lev", "lat"),
    )
    return jax.shard_map(
        functools.partial(per_device, mesh.shape["lev"], mesh.shape["lat"]),
        mesh=mesh,
        in_specs=placed,
        out_specs=(P(None, "lev", "lat", None), P("lev", "lat", None, None)),
        check_vma=False,
    )
```
